512 devices in a mesh: req: 32 (over x, y_lo, core), mp: 16 (over z, y_hi).
Axes of the slice: x: 4, y: 8 (y_hi: 2, y_lo: 4; y = y_hi * 4 + y_lo), z: 8, core: 2. Of those that a mesh axis runs over, the one named last changes fastest.
Arguments:
- xin: bfloat16 [32, 64, 8192], P('req', None, 'mp'), may hold values from -6 to 6
- zin: bfloat16 [32, 64, 8192], P('req', None, 'mp'), may hold values from -6 to 6
- conv_w: float32 [4, 8192], P(None, 'mp'), may hold values from -3 to 3
- conv_bias: float32 [8192], P('mp'), may hold values from -3 to 3
- x_proj: bfloat16 [8192, 288], P('mp'), may hold values from -0.0625 to 0.0625
- dt_proj: bfloat16 [256, 8192], P(None, 'mp'), may hold values from -0.375 to 0.375
- dt_bias: float32 [8192], P('mp'), may hold values from -5 to -2
- a_log: float32 [16, 8192], P(None, 'mp'), may hold values from 0 to 2.8
- d_skip: float32 [8192], P('mp'), may hold values from 0.5 to 1.5
- conv_cache: float32 [64, 3, 8192], P('req', None, 'mp'), may hold values from -6 to 6
- ssm_cache: float32 [64, 16, 8192], P('req', None, 'mp'), may hold values from -3 to 3
- prefix_of: int32 [32], replicated, may hold values from 0 to 63, as said below
- out_w: bfloat16 [8192, 4096], P('mp', 'req'), may hold values from -0.0625 to 0.0625
- resid: bfloat16 [2048, 4096], P(('req', 'mp')), may hold values from -6 to 6
- norm_gain: float32 [4096], replicated, may hold values from 0.5 to 1.5
- expert_ids: int32 [2048, 2], P('req'), may hold values from 0 to 7, all different within a row; in each aligned block of 4 rows (0 to 3, 4 to 7, ...) at most 2 rows name the same one
- gate_w: bfloat16 [2048, 2], P('req'), may hold values from 0.19921875 to 1
- w_gate: bfloat16 [32, 4096, 4096], P('req', None, 'mp'), may hold values from -0.09375 to 0.09375
- w_up: bfloat16 [32, 4096, 4096], P('req', None, 'mp'), may hold values from -0.09375 to 0.09375
Outputs:
- stream: bfloat16 [2048, 4096], P(('req', 'mp'))
- final_state: float32 [32, 16, 8192], P('req', None, 'mp')
- expert_act: bfloat16 [32, 1024, 4096], P('req', None, 'mp')
The draws below stay inside these ranges and needn't reach their ends.
Inputs may be any that keep to these rules, and one draw needn't show every extreme that they name: `prefix_of`: prefix p is cached on index p // 2 of req. `expert_ids`: within each aligned block of 4 tokens no expert is named more than 2 times; a token's two experts differ.
All inputs are finite; a program needn't handle non-finite values.
Results may differ from the reference program's by a relative error of at most 0.025.
Values may be sent and summed in bfloat16 or wider, within the bound.
A program may use at most 64 MiB of HBM per device.

```python
import math
import jax
import jax.numpy as jnp
import numpy as np
from jax import lax

D = 4096
DI = 8192
NS = 16
CONV = 4
DTR = 256
EXPERTS = 8
PFX_DEV = 2
SUF = 64
TOK_DEV = 4
CAP = 2
TOKENS = 2048
PREFIXES = 64
FF_BLOCK = 4096
SLOTS = 1024
N_REQ = 32
DEVICES = 512


def draw_prefix_of(key, part):
    key = jax.random.fold_in(key, 11)
    owner_key = jax.random.fold_in(key, 1)
    hot_key = jax.random.fold_in(key, 2)
    pick_key = jax.random.fold_in(key, 3)
    slot_key = jax.random.fold_in(key, 4)
    owners = jax.random.randint(owner_key, (N_REQ,), 0, N_REQ, dtype=jnp.int32)
    hot_owner = jax.random.randint(hot_key, (), 0, N_REQ, dtype=jnp.int32)
    to_hot = jax.random.randint(pick_key, (N_REQ,), 0, 3, dtype=jnp.int32) == 0
    owners = jnp.where(to_hot, hot_owner, owners).astype(jnp.int32)
    slots = jax.random.randint(slot_key, (N_REQ,), 0, PFX_DEV, dtype=jnp.int32)
    prefixes = (owners * PFX_DEV + slots).astype(jnp.int32)
    prefixes = prefixes.at[0].set(PREFIXES - 1)
    prefixes = prefixes.at[1].set((1 + N_REQ // 2) % N_REQ * PFX_DEV + slots[1])
    prefixes = prefixes.at[2].set(3 % N_REQ * PFX_DEV + slots[2])
    prefixes = prefixes.at[3].set(0)
    return prefixes.astype(jnp.int32)


def steps_of(stream_key, shape, cuts, least, high):
    def one(axis_at, blocks):
        steps = jax.random.uniform(jax.random.fold_in(jax.random.fold_in(stream_key, 6), axis_at), (blocks,), jnp.float32, least / len(cuts), high / len(cuts))
        return jnp.repeat(jnp.exp(steps), shape[axis_at] // blocks).reshape((-1,) + (1,) * (len(shape) - axis_at - 1))

    gain = one(*cuts[0])
    for cut in cuts[1:]:
        gain = gain * one(*cut)
    return gain


def assign_block(rng, own, number, rows, number_of, top, most, skew):
    sequence = jax.random.permutation(rng, number_of)
    packed, usual = load_shares(number_of, rows * top, most, skew, True), load_shares(number_of, rows * top, most, skew, False)
    places = jnp.arange(number_of)

    def named(tallies, turn):
        used = int((tallies > 0).sum())
        fixed = max(1, used // 4)
        passed = fixed + (places - fixed + turn * (used - fixed)) % max(1, number_of - fixed)
        return jnp.zeros((number_of,), jnp.int32).at[sequence[jnp.where(places < fixed, places, passed)]].set(jnp.asarray(tallies, jnp.int32))

    tallies = jnp.where(number % 4 == 0, named(packed, number // 4), named(usual, number - number // 4 - 1))
    mixed = jax.random.permutation(jax.random.fold_in(own, 3), number_of)
    giver, sink = mixed[0:number_of // 2 * 2:2], mixed[1:number_of // 2 * 2:2]
    margin = jnp.minimum(tallies[giver] - 1, most - tallies[sink]) // 2
    margin = jnp.where((giver == sequence[0]) | (sink == sequence[0]) | (tallies[sink] == 0), 0, jnp.maximum(margin, 0))
    passed = jax.random.randint(jax.random.fold_in(own, 4), (number_of // 2,), 0, 1 << 20) % (margin + 1)
    tallies = tallies.at[giver].add(-passed).at[sink].add(passed)
    members = jnp.searchsorted(jnp.cumsum(tallies), jnp.arange(rows * top), side="right").astype(jnp.int32)
    listing = members.reshape(top, rows).T
    listing = listing[jax.random.permutation(jax.random.fold_in(own, 1), rows)]
    turn = jax.random.randint(jax.random.fold_in(own, 2), (rows, 1), 0, top)
    return jnp.take_along_axis(listing, (jnp.arange(top)[None, :] + turn) % top, axis=1)


def load_shares(amount, total, bound, slope, full):
    portions = [(1 << 20) // math.isqrt(grade ** slope) + 1 for grade in range(1, amount + 1)]
    largest = bound if full else min(bound, max(-(-total // amount), total * portions[0] // sum(portions)))
    least = 1 if total - largest >= amount - 1 else 0
    holding, spare = [largest] + [least] * (amount - 1), total - largest - least * (amount - 1)
    while spare > 0:
        candidates = [i for i in range(1, amount) if holding[i] < largest] or [i for i in range(1, amount) if holding[i] < bound]
        whole, budget = sum([portions[i] for i in candidates]), spare
        for i in candidates:
            addition = min(bound - holding[i], max(1, budget * portions[i] // whole), spare)
            holding[i] = holding[i] + addition
            spare = spare - addition
    return np.array(holding)


def noise(rng, extent, width, bound, pieces=(), kind=jnp.bfloat16):
    factor_of = steps_of(rng, extent, pieces, -0.22, 0.18) if pieces else 1.0
    array = jax.random.normal(rng, extent, jnp.float32) * width * factor_of
    return jnp.minimum(jnp.maximum(array, -bound), bound).astype(kind)


def setup_inputs(seed: int = 0) -> dict:
    arg_keys = jax.random.split(jax.random.key(seed), 20)
    xin = noise(arg_keys[0], (N_REQ, SUF, DI), 1.0, 6.0, ((0, 32), (2, 16)))
    zin = noise(arg_keys[1], (N_REQ, SUF, DI), 1.0, 6.0, ((0, 32), (2, 16)))
    conv_w = noise(arg_keys[2], (CONV, DI), 0.5, 3.0, ((1, 16),), jnp.float32)
    conv_bias = noise(arg_keys[3], (DI,), 0.5, 3.0, ((0, 16),), jnp.float32)
    x_proj = noise(arg_keys[4], (DI, DTR + 2 * NS), DI ** -0.5, 0.0625, ((0, 16),))
    dt_proj = noise(arg_keys[5], (DTR, DI), DTR ** -0.5, 0.375, ((1, 16),))
    dt_bias = jnp.clip(-5.0 + 3.0 * jax.random.uniform(arg_keys[6], (DI,), jnp.float32) ** steps_of(arg_keys[6], (DI,), ((0, 16),), -0.2, 0.2), -5.0, -2.0)
    a_log = jnp.clip(2.8 * jax.random.uniform(arg_keys[7], (NS, DI), jnp.float32) ** steps_of(arg_keys[7], (NS, DI), ((1, 16),), -0.2, 0.2), 0.0, 2.8)
    d_skip = jnp.clip(0.5 + 1.0 * jax.random.uniform(arg_keys[8], (DI,), jnp.float32) ** steps_of(arg_keys[8], (DI,), ((0, 16),), -0.2, 0.2), 0.5, 1.5)
    conv_cache = noise(arg_keys[9], (PREFIXES, CONV - 1, DI), 1.0, 6.0, ((0, 32), (2, 16)), jnp.float32)
    ssm_cache = noise(arg_keys[10], (PREFIXES, NS, DI), 0.5, 3.0, ((0, 32), (2, 16)), jnp.float32)
    prefix_of = draw_prefix_of(jax.random.fold_in(arg_keys[19], 71), 0)
    out_w = noise(arg_keys[12], (DI, D), DI ** -0.5, 0.0625, ((0, 16), (1, 32)))
    resid = noise(arg_keys[13], (TOKENS, D), 1.0, 6.0, ((0, 512),))
    norm_gain = jnp.clip(1.0 + 0.1 * jax.random.normal(arg_keys[14], (D,), jnp.float32), 0.5, 1.5)
    expert_ids_keys = jax.random.split(jax.random.fold_in(arg_keys[15], 1), TOKENS // TOK_DEV)
    expert_ids_turns = jax.random.permutation(jax.random.fold_in(arg_keys[15], 3), TOKENS // TOK_DEV)
    expert_ids = jax.vmap(lambda own, number: assign_block(jax.random.fold_in(arg_keys[15], 2), own, number, TOK_DEV, EXPERTS, 2, CAP, 2))(expert_ids_keys, expert_ids_turns).reshape((TOKENS, 2))
    gate_w = jnp.clip(0.19921875 + 0.80078125 * jax.random.uniform(arg_keys[16], (TOKENS, 2), jnp.float32) ** steps_of(arg_keys[16], (TOKENS, 2), ((0, 32),), -0.2, 0.2), 0.19921875, 1.0).astype(jnp.bfloat16)
    w_gate = noise(arg_keys[17], (N_REQ, D, FF_BLOCK), D ** -0.5, 0.09375, ((0, 32), (2, 16)))
    w_up = noise(arg_keys[18], (N_REQ, D, FF_BLOCK), D ** -0.5, 0.09375, ((0, 32), (2, 16)))
    return {"xin": xin, "zin": zin, "conv_w": conv_w, "conv_bias": conv_bias, "x_proj": x_proj, "dt_proj": dt_proj, "dt_bias": dt_bias, "a_log": a_log, "d_skip": d_skip, "conv_cache": conv_cache, "ssm_cache": ssm_cache, "prefix_of": prefix_of, "out_w": out_w, "resid": resid, "norm_gain": norm_gain, "expert_ids": expert_ids, "gate_w": gate_w, "w_gate": w_gate, "w_up": w_up}


def slot_ranks(ids_rows):
    onehot = (ids_rows[..., None] == jnp.arange(EXPERTS, dtype=jnp.int32)).astype(jnp.int32)
    before = jnp.cumsum(onehot, axis=1) - onehot
    return lax.optimization_barrier(jnp.sum(before * onehot, axis=-1)).astype(jnp.int32)

def reference(xin, zin, conv_w, conv_bias, x_proj, dt_proj, dt_bias, a_log, d_skip, conv_cache, ssm_cache, prefix_of, out_w, resid, norm_gain, expert_ids, gate_w, w_gate, w_up):
    conv_state = conv_cache[prefix_of]
    start_state = ssm_cache[prefix_of]
    xpad = jnp.concatenate([conv_state, xin.astype(jnp.float32)], axis=1)
    total = conv_w[0] * xpad[:, 0:SUF]
    for tap in range(1, CONV):
        total = total + conv_w[tap] * xpad[:, tap:tap + SUF]
    conv = total + conv_bias
    u_act = jax.nn.silu(conv).astype(jnp.bfloat16)
    dbc = jnp.dot(u_act.reshape(-1, DI), x_proj, preferred_element_type=jnp.float32)
    dtin = dbc[:, :DTR].astype(jnp.bfloat16)
    step_size = jax.nn.softplus(jnp.dot(dtin, dt_proj, preferred_element_type=jnp.float32) + dt_bias)
    step_size = step_size.reshape(N_REQ, SUF, DI)
    b_coef = dbc[:, DTR:DTR + NS].reshape(N_REQ, SUF, NS)
    c_coef = dbc[:, DTR + NS:].reshape(N_REQ, SUF, NS)
    amat = -jnp.exp(a_log)
    u_float = u_act.astype(jnp.float32)

    def advance(state, inputs):
        dt_now, b_now, c_now, u_now = inputs
        decay = jnp.exp(dt_now[:, None, :] * amat[None])
        state = decay * state + b_now[:, :, None] * (dt_now * u_now)[:, None, :]
        out_now = lax.optimization_barrier(jnp.sum(c_now[:, :, None] * state, axis=1)) + d_skip * u_now
        return (state, out_now)
    inputs = (jnp.swapaxes(step_size, 0, 1), jnp.swapaxes(b_coef, 0, 1), jnp.swapaxes(c_coef, 0, 1), jnp.swapaxes(u_float, 0, 1))
    final_state, outs = lax.scan(advance, start_state, inputs)
    yv = jnp.swapaxes(outs, 0, 1)
    ymix = (yv * jax.nn.silu(zin.astype(jnp.float32))).astype(jnp.bfloat16)
    hidden = jnp.dot(ymix.reshape(-1, DI), out_w, preferred_element_type=jnp.float32) + resid.astype(jnp.float32)
    stream = hidden.astype(jnp.bfloat16)
    moe_in = (hidden * lax.rsqrt(lax.optimization_barrier(jnp.mean(hidden * hidden, axis=-1, keepdims=True)) + 1e-05) * norm_gain).astype(jnp.bfloat16)
    ids = expert_ids.reshape(DEVICES, 2 * TOK_DEV)
    ranks = slot_ranks(ids)
    positions = (jnp.arange(DEVICES, dtype=jnp.int32)[:, None] * CAP + ranks).astype(jnp.int32)
    pair_index = jnp.arange(TOKENS * 2, dtype=jnp.int32).reshape(DEVICES, 2 * TOK_DEV)
    table = jnp.full((EXPERTS, SLOTS), TOKENS * 2, dtype=jnp.int32).at[ids, positions].set(pair_index)
    rows = jnp.concatenate([jnp.repeat(moe_in, 2, axis=0), jnp.zeros((1, D), jnp.bfloat16)], axis=0)
    gates = jnp.concatenate([gate_w.reshape(-1), jnp.zeros((1,), jnp.bfloat16)], axis=0)
    group = N_REQ // EXPERTS

    def per_row(row):
        index = table[row // group]
        slots_x = rows[index]
        slots_g = gates[index].astype(jnp.float32)
        gate_part = jnp.dot(slots_x, w_gate[row], preferred_element_type=jnp.float32)
        up_part = jnp.dot(slots_x, w_up[row], preferred_element_type=jnp.float32)
        return (jax.nn.silu(gate_part) * up_part * slots_g[:, None]).astype(jnp.bfloat16)
    expert_act = lax.map(per_row, jnp.arange(N_REQ, dtype=jnp.int32))
    return (stream, final_state, expert_act)
```

```python
import jax
import jax.numpy as jnp
from jax import lax
from jax.experimental import pallas as pl
from jax.experimental.pallas import tpu as pltpu
from jax.sharding import PartitionSpec as P

F32 = jnp.float32
BF16 = jnp.bfloat16
MESH = pl.DeviceIdType.MESH

D = 4096
CH = 512
NS = 16
SUF = 64
DTR = 256
EXPERTS = 8
HID = 256
KT = 1024


def iota(shape, dim):
    return lax.broadcasted_iota(jnp.int32, shape, dim)


def silu(v):
    return v / (1.0 + jnp.exp(-v))


def steps_right(g):
    return 4 if g < 2 else 3


def steps_left(g):
    return 3 if g < 2 else 4


def kernel(
    prefix_of,
    xin,
    zin,
    conv_w,
    conv_bias,
    x_proj,
    dt_proj,
    dt_bias,
    a_log,
    d_skip,
    conv_cache,
    ssm_cache,
    out_w,
    resid,
    norm_gain,
    expert_ids,
    gate_w,
    w_gate,
    w_up,
    stream_out,
    state_out,
    act_out,
    cc16,
    cs16,
    xpad,
    a_send,
    a_recv1,
    a_mid,
    a_recv2,
    b_send,
    b_recv1,
    b_mid,
    b_recv2,
    gmat,
    d_send,
    d_recv,
    d_sum,
    d_all,
    dt_s,
    u_s,
    yv_s,
    b_exp,
    c_exp,
    ow,
    pq,
    perm_big,
    perm_small,
    p_send,
    p_recv,
    r4,
    r32,
    h4,
    sel,
    e_send,
    e_mid,
    e_recv,
    xb,
    wg,
    wu,
    acc_g,
    acc_u,
    s_a1,
    r_a1,
    s_a2,
    r_a2,
    s_b1,
    r_b1,
    s_b2,
    r_b2,
    s_d1,
    r_d1,
    s_d2,
    r_d2,
    s_oy,
    r_oy,
    s_ox,
    r_ox,
    s_ox2,
    r_ox2,
    s_os,
    r_os,
    s_p,
    r_p,
    s_ex,
    r_ex,
    s_ey,
    r_ey,
    s_zr,
    r_zr,
    s_zs,
    r_zs,
    loc,
):
    me = lax.axis_index("req")
    mp = lax.axis_index("mp")
    x = me // 8
    ylo = (me // 2) % 4
    core = me % 2
    j = me % 8
    z = mp // 2
    hi = mp % 2
    yy = hi * 4 + ylo

    def req_of(px, pylo, pcore):
        return px * 8 + pylo * 2 + pcore

    def send(src, dst, ssem, rsem, to_req, to_mp):
        return pltpu.make_async_remote_copy(
            src_ref=src,
            dst_ref=dst,
            send_sem=ssem,
            recv_sem=rsem,
            device_id=(to_req, to_mp),
            device_id_type=MESH,
        )

    pending = []

    def go(copy):
        copy.start()
        pending.append(copy)
        return copy

    x_to = {d: req_of((x + d) % 4, ylo, core) for d in (1, 2, 3)}
    j_to = {d: x * 8 + (j + d) % 8 for d in range(1, 8)}
    mp_to = {}
    for dz in range(8):
        for dh in range(2):
            if dz or dh:
                mp_to[dz * 2 + dh] = ((z + dz) % 8) * 2 + (hi + dh) % 2
    y_to = {}
    for d in range(1, 8):
        other = (yy + d) % 8
        y_to[d] = (req_of(x, other % 4, core), z * 2 + other // 4)
    sibling = req_of(x, ylo, 1 - core)

    barrier = pltpu.get_barrier_semaphore()
    count = 0
    for d in (1, 2, 3):
        pl.semaphore_signal(barrier, inc=1, device_id=(x_to[d], mp), device_id_type=MESH)
        count += 1
    for d in range(1, 8):
        pl.semaphore_signal(barrier, inc=1, device_id=(j_to[d], mp), device_id_type=MESH)
        count += 1
    for d in mp_to:
        pl.semaphore_signal(barrier, inc=1, device_id=(me, mp_to[d]), device_id_type=MESH)
        count += 1
    for d in (1, 2, 3):
        to = req_of(x, (ylo + d) % 4, core)
        pl.semaphore_signal(
            barrier, inc=1, device_id=(to, z * 2 + (1 - hi)), device_id_type=MESH
        )
        count += 1

    own_id = core * 16 + x * 4 + ylo
    load_g = pltpu.make_async_copy(w_gate.at[0], wg, loc.at[0])
    load_u = pltpu.make_async_copy(w_up.at[0], wu, loc.at[1])
    load_o = pltpu.make_async_copy(out_w, ow.at[own_id], loc.at[2])
    load_g.start()
    load_u.start()
    load_o.start()

    cc16[...] = jnp.zeros_like(cc16)
    for s in range(2):
        for k in range(3):
            for q in range(4):
                cc16[s, 4 * k + q : 4 * k + q + 1, :] = conv_cache[s, k : k + 1, q * 128 : q * 128 + 128]

    def fill_a(t, _):
        p = prefix_of[t]
        f0 = jnp.where(p == 2 * me, 1.0, 0.0).astype(F32)
        f1 = jnp.where(p == 2 * me + 1, 1.0, 0.0).astype(F32)
        a_send[t // 8, t % 8] = (cc16[0] * f0 + cc16[1] * f1).astype(BF16)
        return 0

    lax.fori_loop(0, 32, fill_a, 0)
    pl.semaphore_wait(barrier, count)

    a1 = {}
    for d in (1, 2, 3):
        a1[d] = go(
            send(
                a_send.at[(x + d) % 4], a_recv1.at[d], s_a1.at[d], r_a1.at[d], x_to[d], mp
            )
        )

    ids = [expert_ids[:, k : k + 1] for k in range(2)]
    gates = [gate_w[:, k : k + 1].astype(F32) for k in range(2)]
    lane8 = iota((SUF, 128), 1)
    onehot = (
        jnp.where(ids[0] == lane8, 1.0, 0.0) + jnp.where(ids[1] == lane8, 1.0, 0.0)
    ).astype(BF16)
    tri_r, tri_c = iota((SUF, SUF), 0), iota((SUF, SUF), 1)
    tri = jnp.where((tri_r // 4 == tri_c // 4) & (tri_c < tri_r), 1.0, 0.0).astype(BF16)
    before = jnp.dot(tri, onehot, preferred_element_type=F32)
    ranks = [
        jnp.sum(jnp.where(ids[k] == lane8, before, 0.0), axis=1, keepdims=True) for k in range(2)
    ]
    token = iota((SUF, 128), 0)
    lane = iota((SUF, 128), 1)
    place = (
        (token // 4 == (lane % 64) // 2)
        & (lane % 64 < 32)
        & (lane // 64 == me % 2)
    )
    lane_rank = (lane % 2).astype(F32)
    row16 = iota((16, 128), 0)

    def fill_g(e, _):
        total = jnp.zeros((1, 128), F32)
        for k in range(2):
            hit = place & (ids[k] == e) & (ranks[k] == lane_rank)
            total = total + jnp.sum(jnp.where(hit, gates[k], 0.0), axis=0, keepdims=True)
        gmat[e] = jnp.where(row16 == me // 2, jnp.broadcast_to(total, (16, 128)), 0.0).astype(BF16)
        return 0

    lax.fori_loop(0, EXPERTS, fill_g, 0)

    def fill_b(t, _):
        p = prefix_of[t]
        f0 = jnp.where(p == 2 * me, 1.0, 0.0).astype(F32)
        f1 = jnp.where(p == 2 * me + 1, 1.0, 0.0).astype(F32)
        b_send[t // 8, t % 8, :, 0:CH] = (ssm_cache[0] * f0 + ssm_cache[1] * f1).astype(BF16)
        b_send[t // 8, t % 8, :, CH : CH + 128] = gmat[t // 4]
        return 0

    lax.fori_loop(0, 32, fill_b, 0)

    for d in (1, 2, 3):
        a1[d].wait_recv()

    def mid_a(i, _):
        total = a_send[x, i].astype(F32)
        for d in (1, 2, 3):
            total = total + a_recv1[d, i].astype(F32)
        a_mid[i] = total.astype(BF16)
        return 0

    lax.fori_loop(0, 8, mid_a, 0)
    a2 = {}
    for d in range(1, 8):
        a2[d] = go(
            send(a_mid.at[(j + d) % 8], a_recv2.at[d], s_a2.at[d], r_a2.at[d], j_to[d], mp)
        )
    b1 = {}
    for d in (1, 2, 3):
        b1[d] = go(
            send(
                b_send.at[(x + d) % 4], b_recv1.at[d], s_b1.at[d], r_b1.at[d], x_to[d], mp
            )
        )

    def ow_id(px, pylo):
        return core * 16 + ((px + 4) % 4) * 4 + (pylo + 4) % 4

    oy = {}
    for d in (1, 2, 3):
        to = req_of(x, (ylo + d) % 4, core)
        oy[d] = go(send(out_w, ow.at[own_id], s_oy.at[d], r_oy.at[d], to, mp))
    ox = {}
    for way, d in ((0, 1), (1, 3)):
        ox[way, 0] = go(
            send(out_w, ow.at[own_id], s_ox.at[way, 0], r_ox.at[way, 0], x_to[d], mp)
        )
    os_ = {(0, 0): go(send(out_w, ow.at[own_id], s_os.at[0, 0], r_os.at[0, 0], sibling, mp))}

    xpad[8 : 8 + SUF, :] = xin[0].astype(F32)
    r4[...] = resid[...].astype(F32)
    for t in range(4):
        for q in range(8):
            r32[t * 8 + q : t * 8 + q + 1, :] = r4[t : t + 1, q * 512 : q * 512 + 512]
    d_send[:, :, 256:384] = jnp.zeros((8, 8, 128), F32)

    for d in range(1, 8):
        a2[d].wait_recv()
    total = a_mid[j].astype(F32)
    for d in range(1, 8):
        total = total + a_recv2[d].astype(F32)
    cs16[...] = total
    for k in range(3):
        for q in range(4):
            xpad[5 + k : 6 + k, q * 128 : q * 128 + 128] = cs16[4 * k + q : 4 * k + q + 1, :]

    conv = conv_w[0:1, :] * xpad[5 : 5 + SUF, :]
    for k in range(1, 4):
        conv = conv + conv_w[k : k + 1, :] * xpad[5 + k : 5 + k + SUF, :]
    conv = conv + conv_bias[...]
    u16 = silu(conv).astype(BF16)
    u_s[...] = u16.astype(F32)
    part = jnp.dot(u16, x_proj[:, 0:DTR], preferred_element_type=F32)
    part_bc = jnp.dot(u16, x_proj[:, DTR : DTR + 2 * NS], preferred_element_type=F32)
    d_send[:, :, 0:DTR] = part.reshape(8, 8, DTR)
    d_send[:, :, DTR : DTR + 2 * NS] = part_bc.reshape(8, 8, 2 * NS)

    d1 = {}
    for rel in mp_to:
        d1[rel] = go(
            send(
                d_send.at[(z + rel // 2) % 8],
                d_recv.at[rel],
                s_d1.at[rel],
                r_d1.at[rel],
                me,
                mp_to[rel],
            )
        )

    for d in (1, 2, 3):
        b1[d].wait_recv()

    def mid_b(i, _):
        total = b_send[x, i].astype(F32)
        for d in (1, 2, 3):
            total = total + b_recv1[d, i].astype(F32)
        b_mid[i] = total.astype(BF16)
        return 0

    lax.fori_loop(0, 8, mid_b, 0)
    b2 = {}
    for d in range(1, 8):
        b2[d] = go(
            send(b_mid.at[(j + d) % 8], b_recv2.at[d], s_b2.at[d], r_b2.at[d], j_to[d], mp)
        )

    for rel in mp_to:
        d1[rel].wait_recv()
    total = d_send[z]
    for rel in mp_to:
        total = total + d_recv[rel]
    d_sum[...] = total
    d_all[z] = total
    d2 = {}
    for dz in range(1, 8):
        d2[dz] = go(
            send(
                d_sum,
                d_all.at[z],
                s_d2.at[dz],
                r_d2.at[dz],
                me,
                ((z + dz) % 8) * 2 + hi,
            )
        )

    for d in (1, 2, 3):
        oy[d].wait_recv()
        block = ow.at[ow_id(x, ylo - d)]
        for way, dx in ((0, 1), (1, 3)):
            ox[way, d] = go(
                send(block, block, s_ox.at[way, d], r_ox.at[way, d], x_to[dx], mp)
            )
        os_[0, d] = go(send(block, block, s_os.at[0, d], r_os.at[0, d], sibling, mp))

    big_r, big_c = iota((512, 512), 0), iota((512, 512), 1)
    perm_big[...] = jnp.where(big_c == (big_r % 8) * 64 + big_r // 8, 1.0, 0.0).astype(BF16)
    small_r, small_c = iota((128, 128), 0), iota((128, 128), 1)
    perm_small[...] = jnp.where(small_c == (small_r % 16) * 8 + small_r // 16, 1.0, 0.0).astype(
        BF16
    )
    tok32 = iota((SUF, 32), 0)
    mine = tok32 == mp * 4 + iota((SUF, 32), 1) // 8
    sel_r, sel_c = iota((128, 32), 0), iota((128, 32), 1)
    chosen = jnp.zeros((128, 32), F32)
    for k in range(2):
        id_row = jnp.sum(jnp.where(mine, ids[k].astype(F32), 0.0), axis=0, keepdims=True)
        rank_row = jnp.sum(jnp.where(mine, ranks[k], 0.0), axis=0, keepdims=True)
        hit = (
            (sel_r % 8 == sel_c % 8)
            & ((sel_r // 16).astype(F32) == id_row)
            & (((sel_r // 8) % 2).astype(F32) == rank_row)
        )
        chosen = chosen + jnp.where(hit, 1.0, 0.0)
    sel[...] = chosen.astype(BF16)

    for dz in range(1, 8):
        d2[dz].wait_recv()
    dbc_in = d_all[:, :, 0:DTR].reshape(SUF, DTR).astype(BF16)
    pre = jnp.dot(dbc_in, dt_proj[...], preferred_element_type=F32) + dt_bias[...]
    dt_s[...] = jnp.maximum(pre, 0.0) + jnp.log1p(jnp.exp(-jnp.abs(pre)))
    mask_b = jnp.where(iota((NS, 128), 1) == iota((NS, 128), 0), 1.0, 0.0)
    mask_c = jnp.where(iota((NS, 128), 1) == iota((NS, 128), 0) + NS, 1.0, 0.0)

    def spread(i, _):
        rows = d_all[i, :, DTR : DTR + 128]
        for t in range(8):
            row = jnp.broadcast_to(rows[t : t + 1, :], (NS, 128))
            b_exp[i * 8 + t] = jnp.broadcast_to(
                jnp.sum(row * mask_b, axis=1, keepdims=True), (NS, 128)
            )
            c_exp[i * 8 + t] = jnp.broadcast_to(
                jnp.sum(row * mask_c, axis=1, keepdims=True), (NS, 128)
            )
        return 0

    lax.fori_loop(0, 8, spread, 0)

    for d in range(1, 8):
        b2[d].wait_recv()
    total = b_mid[j].astype(F32)
    for d in range(1, 8):
        total = total + b_recv2[d].astype(F32)
    gates16 = total[:, CH : CH + 128].astype(BF16)
    amat = -jnp.exp(a_log[...])

    def widen(v):
        return jnp.concatenate([v, v, v, v], axis=1)

    def scan8(i, state):
        dt8 = dt_s[pl.ds(pl.multiple_of(i * 8, 8), 8), :]
        u8 = u_s[pl.ds(pl.multiple_of(i * 8, 8), 8), :]
        du8 = dt8 * u8
        for t in range(8):
            decay = jnp.exp(dt8[t : t + 1, :] * amat)
            state = decay * state + widen(b_exp[i * 8 + t]) * du8[t : t + 1, :]
            yv_s[pl.ds(i * 8 + t, 1), :] = jnp.sum(
                widen(c_exp[i * 8 + t]) * state, axis=0, keepdims=True
            )
        return state

    state = lax.fori_loop(0, 8, scan8, total[:, 0:CH])
    state_out[...] = state

    ox2 = {}
    for k in range(4):
        for way, dx, back in ((0, 1, -1), (1, 3, 1)):
            ox[way, k].wait_recv()
            block = ow.at[ow_id(x + back, ylo - k)]
            if (k < 2) == (way == 0):
                ox2[k] = go(send(block, block, s_ox2.at[k], r_ox2.at[k], x_to[dx], mp))
            os_[1 + way, k] = go(
                send(block, block, s_os.at[1 + way, k], r_os.at[1 + way, k], sibling, mp)
            )

    gated = (yv_s[...] + d_skip[...] * u_s[...]) * silu(zin[0].astype(F32))
    ymix = gated.astype(BF16)

    for k in range(4):
        ox2[k].wait_recv()
        block = ow.at[ow_id(x + 2, ylo - k)]
        os_[3, k] = go(send(block, block, s_os.at[3, k], r_os.at[3, k], sibling, mp))
    load_o.wait()
    for key in os_:
        os_[key].wait_recv()

    def project(q, _):
        cols = jnp.concatenate(
            [ow[2 * q], ow[16 + 2 * q], ow[2 * q + 1], ow[17 + 2 * q]], axis=1
        )
        pq[pl.ds(pl.multiple_of(q * 64, 64), 64), :] = jnp.dot(
            ymix, cols, preferred_element_type=F32
        ).astype(BF16)
        return 0

    lax.fori_loop(0, 8, project, 0)

    def reorder(i, _):
        rows = jnp.dot(
            perm_big[pl.ds(pl.multiple_of(i * 128, 128), 128), :], pq[...], preferred_element_type=F32
        )
        p_send[pl.ds(i * 4, 4)] = rows.astype(BF16).reshape(4, 32, 512)
        return 0

    lax.fori_loop(0, 4, reorder, 0)
    ps = {}
    for rel in mp_to:
        ps[rel] = go(
            send(
                p_send.at[mp_to[rel]],
                p_recv.at[rel],
                s_p.at[rel],
                r_p.at[rel],
                me,
                mp_to[rel],
            )
        )
    hidden = r32[...] + p_send[mp].astype(F32)
    for rel in mp_to:
        ps[rel].wait_recv()
        hidden = hidden + p_recv[rel].astype(F32)

    for t in range(4):
        block = hidden[t * 8 : t * 8 + 8, :]
        square = jnp.sum(jnp.sum(block * block, axis=1, keepdims=True), axis=0, keepdims=True)
        scale = lax.rsqrt(square * (1.0 / D) + 1e-05)
        r32[t * 8 : t * 8 + 8, :] = block * scale * norm_gain[...]
        for q in range(8):
            h4[t : t + 1, q * 512 : q * 512 + 512] = block[q : q + 1, :]
    e_send[...] = (
        jnp.dot(sel[...], r32[...].astype(BF16), preferred_element_type=F32)
        .astype(BF16)
        .reshape(EXPERTS, 16, 512)
    )

    ex = {}
    for d in (1, 2, 3):
        ex[d] = go(
            send(
                e_send.at[pl.ds(2 * ((x + d) % 4), 2)],
                e_mid.at[:, x],
                s_ex.at[d],
                r_ex.at[d],
                x_to[d],
                mp,
            )
        )
    e_mid[0, x] = e_send[2 * x]
    e_mid[1, x] = e_send[2 * x + 1]
    stream_out[...] = h4[...].astype(BF16)
    load_g.wait()
    load_u.wait()
    for d in (1, 2, 3):
        ex[d].wait_recv()
    ey = {}
    for d in (7, 1, 6, 2, 5, 3, 4):
        parity = (((yy + d) % 8) % 4) // 2
        ey[d] = go(
            send(e_mid.at[parity], e_recv.at[d], s_ey.at[d], r_ey.at[d], y_to[d][0], y_to[d][1])
        )
    e_recv[0] = e_mid[ylo // 2]

    def ring(way, s, g):
        if way == 0:
            block, to = (z + 8 - (s - 1)) % 8, (z + 1) % 8
        else:
            block, to = (z + s - 1) % 8, (z + 7) % 8
        ref = xb.at[block, g, core]
        return go(
            send(ref, ref, s_zr.at[way, s, g], r_zr.at[way, s, g], me, to * 2 + hi)
        )

    def share(row, block, g):
        ref = xb.at[block, g, core]
        return go(send(ref, ref, s_zs.at[row, g], r_zs.at[row, g], sibling, mp))

    zr, zs = {}, {}
    for g in range(4):
        if g:
            ey[g].wait_recv()
        ey[7 - g].wait_recv()
        raw = jnp.concatenate(
            [e_recv[g].reshape(64, 512), e_recv[7 - g].reshape(64, 512)], axis=0
        )
        rows = jnp.dot(perm_small[...], raw, preferred_element_type=F32).astype(BF16)
        for q in range(8):
            xb[z, g, core, :, q * 512 : q * 512 + 512] = rows[q * 16 : q * 16 + 16, :]
        zr[0, 1, g] = ring(0, 1, g)
        zr[1, 1, g] = ring(1, 1, g)
        zs[0, g] = share(0, z, g)

    def expert(blocks):
        m = 128 * len(blocks)
        acc_g[0:m, :] = jnp.zeros((m, HID), F32)
        acc_u[0:m, :] = jnp.zeros((m, HID), F32)

        def tile(k, _):
            ks = pl.ds(pl.multiple_of(k * KT, KT), KT)
            left = jnp.concatenate([xb[b, :, :, :, ks].reshape(128, KT) for b in blocks], axis=0)
            acc_g[0:m, :] += jnp.dot(left, wg[ks, :], preferred_element_type=F32)
            acc_u[0:m, :] += jnp.dot(left, wu[ks, :], preferred_element_type=F32)
            return 0

        lax.fori_loop(0, D // KT, tile, 0)
        i_row = iota((128, 128), 0)
        i_lane = iota((128, 128), 1)
        grp, cc, yi, xs, kk = (
            i_row // 32,
            (i_row // 16) % 2,
            (i_row // 8) % 2,
            (i_row // 2) % 4,
            i_row % 2,
        )
        source = (yy + jnp.where(yi == 0, 8 - grp, grp + 1)) % 8
        pick = jnp.where(iota((128, 16), 1) == (xs * 4 + source % 4)[:, 0:16], 1.0, 0.0).astype(BF16)
        spread_g = jnp.dot(pick, gates16, preferred_element_type=F32)
        for n, b in enumerate(blocks):
            here = i_lane == cc * 64 + b * 4 + (source // 4) * 2 + kk
            weight = jnp.sum(jnp.where(here, spread_g, 0.0), axis=1, keepdims=True)
            rows = slice(n * 128, n * 128 + 128)
            act = silu(acc_g[rows, :]) * acc_u[rows, :] * weight
            for gi in range(4):
                for c in range(2):
                    for yi_ in range(2):
                        off = (8 - gi) % 8 if yi_ == 0 else gi + 1
                        at = gi * 32 + c * 16 + yi_ * 8
                        act_out[b, (yy + off) % 8, c] = act[at : at + 8, :]

    for s in range(1, 5):
        for g in range(4):
            if s <= steps_right(g):
                zr[0, s, g].wait_recv()
                if s + 1 <= steps_right(g):
                    zr[0, s + 1, g] = ring(0, s + 1, g)
                zs[2 * s - 1, g] = share(2 * s - 1, (z + 8 - s) % 8, g)
            if s <= steps_left(g):
                zr[1, s, g].wait_recv()
                if s + 1 <= steps_left(g):
                    zr[1, s + 1, g] = ring(1, s + 1, g)
                row = 2 * s if s < 4 else 7
                zs[row, g] = share(row, (z + s) % 8, g)
        if s == 1:
            for g in range(4):
                zs[0, g].wait_recv()
            expert([z])
        else:
            for g in range(4):
                zs[2 * s - 3, g].wait_recv()
                zs[2 * s - 2, g].wait_recv()
            expert([(z + 9 - s) % 8, (z + s - 1) % 8])
    for g in range(4):
        zs[7, g].wait_recv()
    expert([(z + 4) % 8])

    for copy in pending:
        copy.wait_send()


def local(
    xin,
    zin,
    conv_w,
    conv_bias,
    x_proj,
    dt_proj,
    dt_bias,
    a_log,
    d_skip,
    conv_cache,
    ssm_cache,
    prefix_of,
    out_w,
    resid,
    norm_gain,
    expert_ids,
    gate_w,
    w_gate,
    w_up,
):
    vmem = pl.BlockSpec(memory_space=pltpu.VMEM)
    smem = pl.BlockSpec(memory_space=pltpu.SMEM)
    hbm = pl.BlockSpec(memory_space=pl.ANY)
    dma = pltpu.SemaphoreType.DMA
    v = pltpu.VMEM
    scratch = [
        v((2, 16, 128), F32),
        v((16, 128), F32),
        v((72, CH), F32),
        v((4, 8, 16, 128), BF16),
        v((4, 8, 16, 128), BF16),
        v((8, 16, 128), BF16),
        v((8, 16, 128), BF16),
        v((4, 8, 16, CH + 128), BF16),
        v((4, 8, 16, CH + 128), BF16),
        v((8, 16, CH + 128), BF16),
        v((8, 16, CH + 128), BF16),
        v((8, 16, 128), BF16),
        v((8, 8, 384), F32),
        v((16, 8, 384), F32),
        v((8, 384), F32),
        v((8, 8, 384), F32),
        v((SUF, CH), F32),
        v((SUF, CH), F32),
        v((SUF, CH), F32),
        v((SUF, NS, 128), F32),
        v((SUF, NS, 128), F32),
        v((32, CH, 128), BF16),
        v((512, 512), BF16),
        v((512, 512), BF16),
        v((128, 128), BF16),
        v((16, 32, 512), BF16),
        v((16, 32, 512), BF16),
        v((4, D), F32),
        v((32, 512), F32),
        v((4, D), F32),
        v((128, 32), BF16),
        v((8, 16, 512), BF16),
        v((2, 4, 16, 512), BF16),
        v((8, 4, 16, 512), BF16),
        v((8, 4, 2, 16, D), BF16),
        v((D, HID), BF16),
        v((D, HID), BF16),
        v((256, HID), F32),
        v((256, HID), F32),
    ]
    sems = []
    for shape in (
        (4,),
        (8,),
        (4,),
        (8,),
        (16,),
        (8,),
        (4,),
        (2, 4),
        (4,),
        (4, 4),
        (16,),
        (4,),
        (8,),
        (2, 5, 4),
        (8, 4),
    ):
        sems += [dma(shape), dma(shape)]
    sems.append(dma((3,)))
    stream, state, act = pl.pallas_call(
        kernel,
        out_shape=(
            jax.ShapeDtypeStruct((4, D), BF16),
            jax.ShapeDtypeStruct((NS, CH), F32),
            jax.ShapeDtypeStruct((8, 8, 2, 8, HID), F32),
        ),
        in_specs=[smem] + [vmem] * 11 + [hbm] + [vmem] * 4 + [hbm] * 2,
        out_specs=(vmem, vmem, vmem),
        scratch_shapes=scratch + sems,
        compiler_params=pltpu.CompilerParams(
            collective_id=0, has_side_effects=True, vmem_limit_bytes=48 * 1024 * 1024
        ),
        name="mixer_and_experts",
    )(
        prefix_of,
        xin,
        zin,
        conv_w,
        conv_bias.reshape(1, CH),
        x_proj,
        dt_proj,
        dt_bias.reshape(1, CH),
        a_log,
        d_skip.reshape(1, CH),
        conv_cache,
        ssm_cache,
        out_w,
        resid,
        norm_gain.reshape(8, 512),
        expert_ids,
        gate_w,
        w_gate,
        w_up,
    )
    act = act.reshape(8, 2, 4, 2, 4, 2, HID).transpose(4, 2, 3, 0, 1, 5, 6)
    return (stream, state[None], act.astype(BF16).reshape(1, 1024, HID))


def solution(mesh):
    placed = (
        P("req", None, "mp"),
        P("req", None, "mp"),
        P(None, "mp"),
        P("mp"),
        P("mp", None),
        P(None, "mp"),
        P("mp"),
        P(None, "mp"),
        P("mp"),
        P("req", None, "mp"),
        P("req", None, "mp"),
        P(),
        P("mp", "req"),
        P(("req", "mp"), None),
        P(),
        P("req", None),
        P("req", None),
        P("req", None, "mp"),
        P("req", None, "mp"),
    )
    return jax.shard_map(
        local,
        mesh=mesh,
        in_specs=placed,
        out_specs=(P(("req", "mp"), None), P("req", None, "mp"), P("req", None, "mp")),
        check_vma=False,
    )
```

```python
import types

import jax
import jax.numpy as jnp
from jax import lax
from jax.experimental import pallas as pl
from jax.experimental.pallas import tpu as pltpu
from jax.sharding import PartitionSpec as P

F32 = jnp.float32
BF16 = jnp.bfloat16
MESH = pl.DeviceIdType.MESH

D = 4096
CH = 512
NS = 16
SUF = 64
DTR = 256
EXPERTS = 8
HID = 256
KT = 1024

VMEM = pltpu.VMEM
LOADED = {
    "prefix_of": pltpu.SMEM((32,), jnp.int32),
    "conv_cache": VMEM((3, 2, CH), F32),
    "ids": VMEM((2, SUF), jnp.int32),
    "gate_w": VMEM((2, SUF), BF16),
    "ssm_cache": VMEM((2, NS, CH), F32),
    "xin": VMEM((1, SUF, CH), BF16),
    "conv_w": VMEM((4, CH), F32),
    "conv_bias": VMEM((1, CH), F32),
    "x_proj": VMEM((DTR + 2 * NS, CH), BF16),
    "resid": VMEM((4, D), BF16),
    "norm_gain": VMEM((32, 128), F32),
    "dt_proj": VMEM((DTR, CH), BF16),
    "dt_bias": VMEM((1, CH), F32),
    "a_log": VMEM((NS, CH), F32),
    "d_skip": VMEM((1, CH), F32),
    "zin": VMEM((1, SUF, CH), BF16),
    "w_gate": VMEM((1, D, HID), BF16),
    "w_up": VMEM((1, D, HID), BF16),
}
SCRATCH = {
    "cc16": VMEM((2, 16, 128), F32),
    "cs16": VMEM((16, 128), F32),
    "xpad": VMEM((72, CH), F32),
    "a_send": VMEM((4, 8, 16, 128), BF16),
    "a_recv1": VMEM((4, 8, 16, 128), BF16),
    "a_mid": VMEM((8, 16, 128), BF16),
    "a_recv2": VMEM((8, 16, 128), BF16),
    "b_send": VMEM((4, 8, 16, CH + 128), BF16),
    "b_recv1": VMEM((4, 8, 16, CH + 128), BF16),
    "b_mid": VMEM((8, 16, CH + 128), BF16),
    "b_recv2": VMEM((8, 16, CH + 128), BF16),
    "gmat": VMEM((8, 16, 128), BF16),
    "d_send": VMEM((8, 8, 384), F32),
    "d_recv": VMEM((16, 8, 384), F32),
    "d_sum": VMEM((8, 384), F32),
    "d_all": VMEM((8, 8, 384), F32),
    "dt_s": VMEM((SUF, CH), F32),
    "u_s": VMEM((SUF, CH), F32),
    "yv_s": VMEM((SUF, CH), F32),
    "b_exp": VMEM((SUF, NS, 128), F32),
    "c_exp": VMEM((SUF, NS, 128), F32),
    "ow": VMEM((8, CH, 128), BF16),
    "ymix": VMEM((SUF, CH), BF16),
    "yfull": VMEM((4, SUF, CH), BF16),
    "perm_rows": VMEM((256, 256), BF16),
    "perm_small": VMEM((128, 128), BF16),
    "p_send": VMEM((16, 16, 1024), BF16),
    "p_recv": VMEM((16, 16, 1024), BF16),
    "p_sum": VMEM((16, 1024), F32),
    "hx_send": VMEM((4, 8, 512), F32),
    "hx_recv": VMEM((4, 8, 512), F32),
    "r4": VMEM((4, D), F32),
    "r32": VMEM((4, 8, 512), F32),
    "g8": VMEM((8, 512), F32),
    "g32": VMEM((4, 8, 512), F32),
    "n32": VMEM((32, 512), BF16),
    "h4": VMEM((4, D), F32),
    "sel": VMEM((128, 32), BF16),
    "e_send": VMEM((8, 16, 512), BF16),
    "e_mid": VMEM((2, 4, 16, 512), BF16),
    "e_recv": VMEM((3, 2, 4, 16, 512), BF16),
    "xb": VMEM((8, 4, 2, 16, D), BF16),
    "acc_g": VMEM((256, HID), F32),
    "acc_u": VMEM((256, HID), F32),
}
COPIES = {
    "a1": (4,),
    "a2": (8,),
    "b1": (4,),
    "b2": (8,),
    "d1": (16,),
    "d2": (8,),
    "oy": (4,),
    "os": (4,),
    "yx": (4,),
    "p": (16,),
    "hx": (4,),
    "ex": (4,),
    "ey": (6,),
    "zr": (2, 5, 3),
    "z4": (1,),
    "pr": (8,),
    "zs": (8, 4),
}
OPERANDS = list(LOADED) + ["out_w"]
BUFFERS = list(LOADED) + list(SCRATCH)


def iota(shape, dim):
    return lax.broadcasted_iota(jnp.int32, shape, dim)


def silu(v):
    return v / (1.0 + jnp.exp(-v))


def kernel(*refs):
    hbm = dict(zip(OPERANDS, refs))
    refs = refs[len(OPERANDS) :]
    stream_out, state_out, act_out = refs[:3]
    refs = refs[3:]
    b = types.SimpleNamespace(**dict(zip(BUFFERS, refs)))
    refs = refs[len(BUFFERS) :]
    sems = {name: (refs[2 * n], refs[2 * n + 1]) for n, name in enumerate(COPIES)}
    loc = refs[2 * len(COPIES)]

    me = lax.axis_index("req")
    mp = lax.axis_index("mp")
    x = me // 8
    ylo = (me // 2) % 4
    core = me % 2
    j = me % 8
    z = mp // 2
    hi = mp % 2
    yy = hi * 4 + ylo
    odd = ylo % 2
    pair = yy // 2

    def req_of(px, pylo, pcore):
        return px * 8 + pylo * 2 + pcore

    pending = []

    def send(name, at, src, dst, to_req, to_mp):
        copy = pltpu.make_async_remote_copy(
            src_ref=src,
            dst_ref=dst,
            send_sem=sems[name][0].at[at],
            recv_sem=sems[name][1].at[at],
            device_id=(to_req, to_mp),
            device_id_type=MESH,
        )
        copy.start()
        pending.append(copy)
        return copy

    loads = {}
    for n, name in enumerate(LOADED):
        loads[name] = pltpu.make_async_copy(hbm[name], getattr(b, name), loc.at[n])
        loads[name].start()
    load_o = pltpu.make_async_copy(hbm["out_w"], b.ow.at[j], loc.at[len(LOADED)])
    load_o.start()

    x_to = {d: req_of((x + d) % 4, ylo, core) for d in (1, 2, 3)}
    j_to = {d: x * 8 + (j + d) % 8 for d in range(1, 8)}
    mp_to = {}
    for dz in range(8):
        for dh in range(2):
            if dz or dh:
                mp_to[dz * 2 + dh] = ((z + dz) % 8) * 2 + (hi + dh) % 2
    sibling = req_of(x, ylo, 1 - core)
    partner = req_of(x, ylo + 1 - 2 * odd, core)

    barrier = pltpu.get_barrier_semaphore()
    greet = [(x_to[d], mp) for d in x_to]
    greet += [(j_to[d], mp) for d in j_to]
    greet += [(me, mp_to[d]) for d in mp_to]
    greet += [(req_of(x, (ylo + d) % 4, core), z * 2 + 1 - hi) for d in (1, 2, 3)]
    for to in greet:
        pl.semaphore_signal(barrier, inc=1, device_id=to, device_id_type=MESH)

    b.cc16[...] = jnp.zeros_like(b.cc16)
    loads["prefix_of"].wait()
    loads["conv_cache"].wait()
    for s in range(2):
        for k in range(3):
            for q in range(4):
                at = 4 * k + q
                b.cc16[s, at : at + 1, :] = b.conv_cache[k, s : s + 1, q * 128 : q * 128 + 128]

    def owned(t):
        p = b.prefix_of[t]
        f0 = jnp.where(p == 2 * me, 1.0, 0.0).astype(F32)
        f1 = jnp.where(p == 2 * me + 1, 1.0, 0.0).astype(F32)
        return f0, f1

    def fill_a(t, _):
        f0, f1 = owned(t)
        b.a_send[t // 8, t % 8] = (b.cc16[0] * f0 + b.cc16[1] * f1).astype(BF16)
        return 0

    lax.fori_loop(0, 32, fill_a, 0)
    pl.semaphore_wait(barrier, len(greet))

    a1 = {d: send("a1", d, b.a_send.at[(x + d) % 4], b.a_recv1.at[d], x_to[d], mp) for d in x_to}
    oy = {}
    for d in (1, 2, 3):
        to = req_of(x, (ylo + d) % 4, core)
        oy[d] = send("oy", d, hbm["out_w"], b.ow.at[j], to, mp)
    osib = {0: send("os", 0, hbm["out_w"], b.ow.at[j], sibling, mp)}

    loads["ids"].wait()
    loads["gate_w"].wait()
    eye = iota((SUF, SUF), 0) == iota((SUF, SUF), 1)

    def column(row):
        return jnp.sum(jnp.where(eye, row, 0.0), axis=1, keepdims=True)

    id_rows = b.ids[...].astype(F32)
    gate_rows = b.gate_w[...].astype(F32)
    ids = [column(id_rows[k : k + 1, :]) for k in range(2)]
    gates = [column(gate_rows[k : k + 1, :]) for k in range(2)]
    lane8 = iota((SUF, 128), 1).astype(F32)
    onehot = (
        jnp.where(ids[0] == lane8, 1.0, 0.0) + jnp.where(ids[1] == lane8, 1.0, 0.0)
    ).astype(BF16)
    tri_r, tri_c = iota((SUF, SUF), 0), iota((SUF, SUF), 1)
    tri = jnp.where((tri_r // 4 == tri_c // 4) & (tri_c < tri_r), 1.0, 0.0).astype(BF16)
    before = jnp.dot(tri, onehot, preferred_element_type=F32)
    ranks = [
        jnp.sum(jnp.where(ids[k] == lane8, before, 0.0), axis=1, keepdims=True) for k in range(2)
    ]
    lane = iota((1, 128), 1)
    lane_block = jnp.where((lane % 64 < 32) & (lane // 64 == core), (lane % 64) // 2, -1)
    place = iota((SUF, 1), 0) // 4 == lane_block
    lane_rank = (lane % 2).astype(F32)
    row16 = iota((16, 128), 0)

    def fill_g(e, _):
        total = jnp.zeros((1, 128), F32)
        for k in range(2):
            hit = place & (ids[k] == e.astype(F32)) & (ranks[k] == lane_rank)
            total = total + jnp.sum(jnp.where(hit, gates[k], 0.0), axis=0, keepdims=True)
        b.gmat[e] = jnp.where(row16 == me // 2, jnp.broadcast_to(total, (16, 128)), 0.0).astype(
            BF16
        )
        return 0

    lax.fori_loop(0, EXPERTS, fill_g, 0)
    loads["ssm_cache"].wait()

    def fill_b(t, _):
        f0, f1 = owned(t)
        b.b_send[t // 8, t % 8, :, 0:CH] = (b.ssm_cache[0] * f0 + b.ssm_cache[1] * f1).astype(BF16)
        b.b_send[t // 8, t % 8, :, CH : CH + 128] = b.gmat[t // 4]
        return 0

    lax.fori_loop(0, 32, fill_b, 0)

    for d in x_to:
        a1[d].wait_recv()

    def mid_a(i, _):
        total = b.a_send[x, i].astype(F32)
        for d in (1, 2, 3):
            total = total + b.a_recv1[d, i].astype(F32)
        b.a_mid[i] = total.astype(BF16)
        return 0

    lax.fori_loop(0, 8, mid_a, 0)
    a2 = {d: send("a2", d, b.a_mid.at[(j + d) % 8], b.a_recv2.at[d], j_to[d], mp) for d in j_to}
    b1 = {d: send("b1", d, b.b_send.at[(x + d) % 4], b.b_recv1.at[d], x_to[d], mp) for d in x_to}

    loads["xin"].wait()
    b.xpad[8 : 8 + SUF, :] = b.xin[0].astype(F32)
    b.d_send[:, :, 256:384] = jnp.zeros((8, 8, 128), F32)
    for name in ("conv_w", "conv_bias", "x_proj"):
        loads[name].wait()

    for d in j_to:
        a2[d].wait_recv()
    total = b.a_mid[j].astype(F32)
    for d in j_to:
        total = total + b.a_recv2[d].astype(F32)
    b.cs16[...] = total
    for k in range(3):
        for q in range(4):
            at = 4 * k + q
            b.xpad[5 + k : 6 + k, q * 128 : q * 128 + 128] = b.cs16[at : at + 1, :]

    conv = b.conv_w[0:1, :] * b.xpad[5 : 5 + SUF, :]
    for k in range(1, 4):
        conv = conv + b.conv_w[k : k + 1, :] * b.xpad[5 + k : 5 + k + SUF, :]
    conv = conv + b.conv_bias[...]
    u16 = silu(conv).astype(BF16)
    b.u_s[...] = u16.astype(F32)
    rows_by_rows = (((1,), (1,)), ((), ()))
    part = lax.dot_general(u16, b.x_proj[0:DTR, :], rows_by_rows, preferred_element_type=F32)
    part_bc = lax.dot_general(
        u16, b.x_proj[DTR : DTR + 2 * NS, :], rows_by_rows, preferred_element_type=F32
    )
    b.d_send[:, :, 0:DTR] = part.reshape(8, 8, DTR)
    b.d_send[:, :, DTR : DTR + 2 * NS] = part_bc.reshape(8, 8, 2 * NS)

    d1 = {
        rel: send("d1", rel, b.d_send.at[(z + rel // 2) % 8], b.d_recv.at[rel], me, mp_to[rel])
        for rel in mp_to
    }

    for d in x_to:
        b1[d].wait_recv()

    def mid_b(i, _):
        total = b.b_send[x, i].astype(F32)
        for d in (1, 2, 3):
            total = total + b.b_recv1[d, i].astype(F32)
        b.b_mid[i] = total.astype(BF16)
        return 0

    lax.fori_loop(0, 8, mid_b, 0)
    b2 = {d: send("b2", d, b.b_mid.at[(j + d) % 8], b.b_recv2.at[d], j_to[d], mp) for d in j_to}

    for rel in mp_to:
        d1[rel].wait_recv()
    total = b.d_send[z]
    for rel in mp_to:
        total = total + b.d_recv[rel]
    b.d_sum[...] = total
    b.d_all[z] = total
    d2 = {
        dz: send("d2", dz, b.d_sum, b.d_all.at[z], me, ((z + dz) % 8) * 2 + hi)
        for dz in range(1, 8)
    }

    for d in (1, 2, 3):
        oy[d].wait_recv()
        block = b.ow.at[((ylo + 4 - d) % 4) * 2 + core]
        osib[d] = send("os", d, block, block, sibling, mp)

    row = iota((256, 1), 0)
    target = ((row // 4) % 4) * 64 + (row // 16) * 4 + row % 4
    b.perm_rows[...] = jnp.where(iota((256, 256), 1) == target, 1.0, 0.0).astype(BF16)
    row = iota((128, 1), 0)
    target = (row % 16) * 8 + row // 16
    b.perm_small[...] = jnp.where(iota((128, 128), 1) == target, 1.0, 0.0).astype(BF16)
    col = iota((1, 32), 1)
    mine = iota((SUF, 1), 0) == mp * 4 + (col // 2) % 4
    col_group = (col // 8) * 2 + col % 2
    chosen = jnp.zeros((128, 32), F32)
    for k in range(2):
        id_row = jnp.sum(jnp.where(mine, ids[k], 0.0), axis=0, keepdims=True)
        rank_row = jnp.sum(jnp.where(mine, ranks[k], 0.0), axis=0, keepdims=True)
        hit = (
            (row % 8 == col_group)
            & ((row // 16).astype(F32) == id_row)
            & (((row // 8) % 2).astype(F32) == rank_row)
        )
        chosen = chosen + jnp.where(hit, 1.0, 0.0)
    b.sel[...] = chosen.astype(BF16)
    loads["resid"].wait()
    loads["norm_gain"].wait()
    b.r4[...] = b.resid[...].astype(F32)
    for q in range(8):
        for part_ in range(4):
            at = q * 4 + part_
            b.g8[q : q + 1, part_ * 128 : part_ * 128 + 128] = b.norm_gain[at : at + 1, :]
    for px in range(4):
        for t in range(4):
            for half in range(2):
                at, q = t * 2 + half, px * 2 + half
                b.r32[px, at : at + 1, :] = b.r4[t : t + 1, q * 512 : q * 512 + 512]
                b.g32[px, at : at + 1, :] = b.g8[q : q + 1, :]

    for name in ("dt_proj", "dt_bias", "a_log", "d_skip", "zin"):
        loads[name].wait()
    for dz in d2:
        d2[dz].wait_recv()
    dbc_in = b.d_all[:, :, 0:DTR].reshape(SUF, DTR).astype(BF16)
    pre = jnp.dot(dbc_in, b.dt_proj[...], preferred_element_type=F32) + b.dt_bias[...]
    b.dt_s[...] = jnp.maximum(pre, 0.0) + jnp.log1p(jnp.exp(-jnp.abs(pre)))
    mask_b = jnp.where(iota((NS, 128), 1) == iota((NS, 128), 0), 1.0, 0.0)
    mask_c = jnp.where(iota((NS, 128), 1) == iota((NS, 128), 0) + NS, 1.0, 0.0)

    def spread(i, _):
        rows = b.d_all[i, :, DTR : DTR + 128]
        for t in range(8):
            one = jnp.broadcast_to(rows[t : t + 1, :], (NS, 128))
            b.b_exp[i * 8 + t] = jnp.broadcast_to(
                jnp.sum(one * mask_b, axis=1, keepdims=True), (NS, 128)
            )
            b.c_exp[i * 8 + t] = jnp.broadcast_to(
                jnp.sum(one * mask_c, axis=1, keepdims=True), (NS, 128)
            )
        return 0

    lax.fori_loop(0, 8, spread, 0)

    for d in j_to:
        b2[d].wait_recv()
    total = b.b_mid[j].astype(F32)
    for d in j_to:
        total = total + b.b_recv2[d].astype(F32)
    gates16 = total[:, CH : CH + 128].astype(BF16)
    amat = -jnp.exp(b.a_log[...])

    def widen(v):
        return jnp.concatenate([v, v, v, v], axis=1)

    def scan8(i, state):
        at = pl.ds(pl.multiple_of(i * 8, 8), 8)
        dt8 = b.dt_s[at, :]
        du8 = dt8 * b.u_s[at, :]
        for t in range(8):
            decay = jnp.exp(dt8[t : t + 1, :] * amat)
            state = decay * state + widen(b.b_exp[i * 8 + t]) * du8[t : t + 1, :]
            b.yv_s[pl.ds(i * 8 + t, 1), :] = jnp.sum(
                widen(b.c_exp[i * 8 + t]) * state, axis=0, keepdims=True
            )
        return state

    state = lax.fori_loop(0, 8, scan8, total[:, 0:CH])
    gated = (b.yv_s[...] + b.d_skip[...] * b.u_s[...]) * silu(b.zin[0].astype(F32))
    ymix = gated.astype(BF16)
    b.ymix[...] = ymix
    b.yfull[x] = ymix

    yx = {d: send("yx", d, b.ymix, b.yfull.at[x], x_to[d], mp) for d in x_to}
    state_out[...] = state
    load_o.wait()
    for d in osib:
        osib[d].wait_recv()
    for d in x_to:
        yx[d].wait_recv()
    left = jnp.dot(
        b.perm_rows[...], b.yfull[...].reshape(256, CH), preferred_element_type=F32
    ).astype(BF16)
    for n in range(4):
        cols = jnp.concatenate([b.ow[2 * n], b.ow[2 * n + 1]], axis=1)
        part = jnp.dot(left, cols, preferred_element_type=F32).astype(BF16)
        b.p_send[:, :, n * 256 : n * 256 + 256] = part.reshape(16, 16, 256)
    ps = {
        rel: send("p", rel, b.p_send.at[mp_to[rel]], b.p_recv.at[rel], me, mp_to[rel])
        for rel in mp_to
    }
    total = b.p_send[mp].astype(F32)
    for rel in mp_to:
        ps[rel].wait_recv()
        total = total + b.p_recv[rel].astype(F32)
    b.p_sum[...] = total
    for px in range(4):
        for t in range(4):
            for half in range(2):
                at = t * 2 + half
                b.hx_send[px, at : at + 1, :] = b.p_sum[
                    px * 4 + t : px * 4 + t + 1, half * 512 : half * 512 + 512
                ]
    hx = {d: send("hx", d, b.hx_send.at[(x + d) % 4], b.hx_recv.at[x], x_to[d], mp) for d in x_to}
    b.hx_recv[x] = b.hx_send[x]
    for d in x_to:
        hx[d].wait_recv()

    hidden = [b.hx_recv[px] + b.r32[px] for px in range(4)]
    square = hidden[0] * hidden[0]
    for px in range(1, 4):
        square = square + hidden[px] * hidden[px]
    square = jnp.sum(square, axis=1, keepdims=True)
    scales = []
    for t in range(4):
        mean = (square[2 * t : 2 * t + 1] + square[2 * t + 1 : 2 * t + 2]) * (1.0 / D)
        scales += [lax.rsqrt(mean + 1e-05)] * 2
    scale = jnp.concatenate([jnp.broadcast_to(v, (1, 512)) for v in scales], axis=0)
    normed = [hidden[px] * scale * b.g32[px] for px in range(4)]
    b.n32[...] = jnp.concatenate(normed, axis=0).astype(BF16)
    b.e_send[...] = (
        jnp.dot(b.sel[...], b.n32[...], preferred_element_type=F32)
        .astype(BF16)
        .reshape(EXPERTS, 16, 512)
    )

    ex = {
        d: send(
            "ex", d, b.e_send.at[pl.ds(2 * ((x + d) % 4), 2)], b.e_mid.at[:, x], x_to[d], mp
        )
        for d in x_to
    }
    b.e_mid[0, x] = b.e_send[2 * x]
    b.e_mid[1, x] = b.e_send[2 * x + 1]
    for px in range(4):
        for t in range(4):
            for half in range(2):
                at, q = t * 2 + half, px * 2 + half
                b.h4[t : t + 1, q * 512 : q * 512 + 512] = hidden[px][at : at + 1, :]
    stream_out[...] = b.h4[...].astype(BF16)
    for d in x_to:
        ex[d].wait_recv()

    kind = pair % 2

    def send_y(slot, to_y, parity):
        return send(
            "ey",
            slot * 2 + odd,
            b.e_mid.at[parity],
            b.e_recv.at[slot, odd],
            req_of(x, to_y % 4, core),
            z * 2 + to_y // 4,
        )

    send_y(0, yy + 1 - 2 * odd, kind)
    send_y(1, 2 * ((pair + 1) % 4), 1 - kind)
    send_y(1, 2 * ((pair + 3) % 4) + 1, 1 - kind)
    send_y(2, 2 * ((pair + 2) % 4), kind)
    send_y(2, 2 * ((pair + 2) % 4) + 1, kind)
    b.e_recv[0, odd] = b.e_mid[kind]

    def got_y(slot, member):
        pltpu.make_async_remote_copy(
            src_ref=b.e_mid.at[0],
            dst_ref=b.e_recv.at[slot, member],
            send_sem=sems["ey"][0].at[slot * 2 + member],
            recv_sem=sems["ey"][1].at[slot * 2 + member],
            device_id=(me, mp),
            device_id_type=MESH,
        ).wait_recv()

    own_side = 3 - 2 * odd
    chunk = (0, own_side, 2)

    def ring(way, s, i):
        if way == 0:
            block, to = (z + 8 - (s - 1)) % 8, (z + 1) % 8
        else:
            block, to = (z + s - 1) % 8, (z + 7) % 8
        ref = b.xb.at[block, chunk[i], core]
        return send("zr", (way, s, i), ref, ref, me, to * 2 + hi)

    def in_ring(way, s, i):
        return s <= 3 or (s == 4 and i == way)

    def share(row, block, i):
        ref = b.xb.at[block, chunk[i] if i < 3 else 4 - own_side, core]
        return send("zs", (row, i), ref, ref, sibling, mp)

    def to_pair(row, block):
        ref = b.xb.at[block, own_side, core]
        return send("pr", row, ref, ref, partner, mp)

    block_of = {0: z, 7: (z + 4) % 8}
    for s in (1, 2, 3):
        block_of[2 * s - 1] = (z + 8 - s) % 8
        block_of[2 * s] = (z + s) % 8

    zr, zs, pr = {}, {}, {}
    for i in range(3):
        if i == 0:
            got_y(0, 1 - odd)
        else:
            got_y(i, 0)
            got_y(i, 1)
        raw = b.e_recv[i].reshape(128, 512)
        rows = jnp.dot(b.perm_small[...], raw, preferred_element_type=F32).astype(BF16)
        for q in range(8):
            b.xb[z, chunk[i], core, :, q * 512 : q * 512 + 512] = rows[q * 16 : q * 16 + 16, :]
        zr[0, 1, i] = ring(0, 1, i)
        zr[1, 1, i] = ring(1, 1, i)
        zs[0, i] = share(0, z, i)
        if i == 1:
            pr[0] = to_pair(0, z)

    def handle(s, i):
        for way in (0, 1):
            if (way, s, i) not in zr:
                continue
            zr[way, s, i].wait_recv()
            if in_ring(way, s + 1, i):
                zr[way, s + 1, i] = ring(way, s + 1, i)
            row = 2 * s - 1 + way if s < 4 else 7
            zs[row, i] = share(row, block_of[row], i)
            if i == 1:
                pr[row] = to_pair(row, block_of[row])

    def from_pair(rows):
        for row in rows:
            pr[row].wait_recv()
            zs[row, 3] = share(row, block_of[row], 3)

    i_row = iota((128, 1), 0)
    grp, cc, yi, xs, kk = (
        i_row // 32,
        (i_row // 16) % 2,
        (i_row // 8) % 2,
        (i_row // 2) % 4,
        i_row % 2,
    )
    source = (2 * pair + 2 * grp + yi) % 8
    pick = jnp.where(iota((128, 16), 1) == xs * 4 + source % 4, 1.0, 0.0).astype(BF16)
    spread_g = jnp.dot(pick, gates16, preferred_element_type=F32)
    gate_lane = cc * 64 + (source // 4) * 2 + kk

    def expert(rows):
        for row in rows:
            for i in range(4):
                zs[row, i].wait_recv()
        blocks = [block_of[row] for row in rows]
        m = 128 * len(blocks)
        b.acc_g[0:m, :] = jnp.zeros((m, HID), F32)
        b.acc_u[0:m, :] = jnp.zeros((m, HID), F32)

        def tile(k, _):
            ks = pl.ds(pl.multiple_of(k * KT, KT), KT)
            slots = jnp.concatenate(
                [b.xb[block, :, :, :, ks].reshape(128, KT) for block in blocks], axis=0
            )
            b.acc_g[0:m, :] += jnp.dot(slots, b.w_gate[0, ks, :], preferred_element_type=F32)
            b.acc_u[0:m, :] += jnp.dot(slots, b.w_up[0, ks, :], preferred_element_type=F32)
            return 0

        lax.fori_loop(0, D // KT, tile, 0)
        for n, block in enumerate(blocks):
            here = iota((128, 128), 1) == gate_lane + block * 4
            weight = jnp.sum(jnp.where(here, spread_g, 0.0), axis=1, keepdims=True)
            part = slice(n * 128, n * 128 + 128)
            act = silu(b.acc_g[part, :]) * b.acc_u[part, :] * weight
            for g in range(4):
                for c in range(2):
                    for member in range(2):
                        at = g * 32 + c * 16 + member * 8
                        act_out[block, (2 * pair + 2 * g + member) % 8, c] = act[at : at + 8, :]

    loads["w_gate"].wait()
    loads["w_up"].wait()
    for s in (1, 2, 3):
        for i in range(3):
            handle(s, i)
        if s == 3:
            ref = b.xb.at[(z + 5 + core * 6) % 8, 2, core]
            z4 = send("z4", 0, ref, ref, me, ((z + 1 + core * 6) % 8) * 2 + hi)
        from_pair([0] if s == 1 else [2 * s - 3, 2 * s - 2])
        if s == 2:
            expert([0])
        if s == 3:
            expert([1, 2])
    handle(4, 0)
    handle(4, 1)
    from_pair([5, 6])
    expert([3, 4])
    z4.wait_recv()
    zs[7, 2] = share(7, block_of[7], 2)
    expert([5, 6])
    from_pair([7])
    expert([7])

    for copy in pending:
        copy.wait_send()


def local(
    xin,
    zin,
    conv_w,
    conv_bias,
    x_proj,
    dt_proj,
    dt_bias,
    a_log,
    d_skip,
    conv_cache,
    ssm_cache,
    prefix_of,
    out_w,
    resid,
    norm_gain,
    expert_ids,
    gate_w,
    w_gate,
    w_up,
):
    operands = {
        "prefix_of": prefix_of,
        "conv_cache": conv_cache.transpose(1, 0, 2),
        "ids": expert_ids.T,
        "gate_w": gate_w.T,
        "ssm_cache": ssm_cache,
        "xin": xin,
        "conv_w": conv_w,
        "conv_bias": conv_bias.reshape(1, CH),
        "x_proj": x_proj.T,
        "resid": resid,
        "norm_gain": norm_gain.reshape(32, 128),
        "dt_proj": dt_proj,
        "dt_bias": dt_bias.reshape(1, CH),
        "a_log": a_log,
        "d_skip": d_skip.reshape(1, CH),
        "zin": zin,
        "w_gate": w_gate,
        "w_up": w_up,
        "out_w": out_w,
    }
    vmem = pl.BlockSpec(memory_space=VMEM)
    dma = pltpu.SemaphoreType.DMA
    sems = []
    for shape in COPIES.values():
        sems += [dma(shape), dma(shape)]
    sems.append(dma((len(LOADED) + 1,)))
    stream, state, act = pl.pallas_call(
        kernel,
        out_shape=(
            jax.ShapeDtypeStruct((4, D), BF16),
            jax.ShapeDtypeStruct((NS, CH), F32),
            jax.ShapeDtypeStruct((8, 8, 2, 8, HID), F32),
        ),
        in_specs=[pl.BlockSpec(memory_space=pltpu.HBM)] * len(OPERANDS),
        out_specs=(vmem, vmem, vmem),
        scratch_shapes=list(LOADED.values()) + list(SCRATCH.values()) + sems,
        compiler_params=pltpu.CompilerParams(
            collective_id=0, has_side_effects=True, vmem_limit_bytes=60 * 1024 * 1024
        ),
        name="mixer_and_experts",
    )(*[operands[name] for name in OPERANDS])
    act = act.reshape(8, 2, 4, 2, 4, 2, HID).transpose(4, 2, 3, 0, 1, 5, 6)
    return (stream, state[None], act.astype(BF16).reshape(1, 1024, HID))


def solution(mesh):
    placed = (
        P("req", None, "mp"),
        P("req", None, "mp"),
        P(None, "mp"),
        P("mp"),
        P("mp", None),
        P(None, "mp"),
        P("mp"),
        P(None, "mp"),
        P("mp"),
        P("req", None, "mp"),
        P("req", None, "mp"),
        P(),
        P("mp", "req"),
        P(("req", "mp"), None),
        P(),
        P("req", None),
        P("req", None),
        P("req", None, "mp"),
        P("req", None, "mp"),
    )
    return jax.shard_map(
        local,
        mesh=mesh,
        in_specs=placed,
        out_specs=(P(("req", "mp"), None), P("req", None, "mp"), P("req", None, "mp")),
        check_vma=False,
    )
```

```python
import types

import jax
import jax.numpy as jnp
from jax import lax
from jax.experimental import pallas as pl
from jax.experimental.pallas import tpu as pltpu
from jax.sharding import PartitionSpec as P

F32 = jnp.float32
BF16 = jnp.bfloat16
MESH = pl.DeviceIdType.MESH

D = 4096
CH = 512
NS = 16
SUF = 64
DTR = 256
EXPERTS = 8
HID = 256
KT = 1024

VMEM = pltpu.VMEM
LOADED = {
    "prefix_of": pltpu.SMEM((32,), jnp.int32),
    "conv_cache": VMEM((3, 2, CH), F32),
    "ids": VMEM((2, SUF), jnp.int32),
    "gate_w": VMEM((2, SUF), BF16),
    "ssm_cache": VMEM((2, NS, CH), F32),
    "xin": VMEM((1, SUF, CH), BF16),
    "conv_w": VMEM((4, CH), F32),
    "conv_bias": VMEM((1, CH), F32),
    "x_proj": VMEM((DTR + 2 * NS, CH), BF16),
    "resid": VMEM((4, D), BF16),
    "norm_gain": VMEM((32, 128), F32),
    "dt_proj": VMEM((DTR, CH), BF16),
    "dt_bias": VMEM((1, CH), F32),
    "a_log": VMEM((NS, CH), F32),
    "d_skip": VMEM((1, CH), F32),
    "zin": VMEM((1, SUF, CH), BF16),
    "w_gate": VMEM((1, D, HID), BF16),
    "w_up": VMEM((1, D, HID), BF16),
}
SCRATCH = {
    "cc16": VMEM((2, 16, 128), F32),
    "cs16": VMEM((16, 128), F32),
    "xpad": VMEM((72, CH), F32),
    "a_send": VMEM((4, 8, 16, 128), BF16),
    "a_recv1": VMEM((4, 8, 16, 128), BF16),
    "a_mid": VMEM((8, 16, 128), BF16),
    "a_recv2": VMEM((8, 16, 128), BF16),
    "b_send": VMEM((4, 8, 16, CH + 128), BF16),
    "b_recv1": VMEM((4, 8, 16, CH + 128), BF16),
    "b_mid": VMEM((8, 16, CH + 128), BF16),
    "b_recv2": VMEM((8, 16, CH + 128), BF16),
    "gmat": VMEM((8, 16, 128), BF16),
    "d_send": VMEM((8, 8, 384), F32),
    "d_recv": VMEM((16, 8, 384), F32),
    "d_sum": VMEM((8, 384), F32),
    "d_all": VMEM((8, 8, 384), F32),
    "l_send": VMEM((8, 128), F32),
    "l_recv": VMEM((16, 8, 128), F32),
    "dt_s": VMEM((SUF, CH), F32),
    "u_s": VMEM((SUF, CH), F32),
    "yv_s": VMEM((SUF, CH), F32),
    "b_exp": VMEM((SUF, NS, 128), F32),
    "c_exp": VMEM((SUF, NS, 128), F32),
    "ow": VMEM((8, CH, 128), BF16),
    "ymix": VMEM((2, 32, CH), BF16),
    "yfull": VMEM((2, 4, 32, CH), BF16),
    "perm_rows": VMEM((128, 128), BF16),
    "perm_out": VMEM((128, 128), BF16),
    "perm_small": VMEM((128, 128), BF16),
    "p_send": VMEM((16, 16, 1024), BF16),
    "p_recv": VMEM((16, 16, 1024), BF16),
    "p_sum": VMEM((16, 1024), F32),
    "hx_send": VMEM((4, 8, 512), F32),
    "hx_recv": VMEM((4, 8, 512), F32),
    "r4": VMEM((4, D), F32),
    "r32": VMEM((4, 8, 512), F32),
    "g8": VMEM((8, 512), F32),
    "g32": VMEM((4, 8, 512), F32),
    "n32": VMEM((32, 512), BF16),
    "h4": VMEM((4, D), F32),
    "sel": VMEM((128, 32), BF16),
    "e_send": VMEM((8, 16, 512), BF16),
    "e_mid": VMEM((2, 4, 16, 512), BF16),
    "e_recv": VMEM((3, 2, 4, 16, 512), BF16),
    "xb": VMEM((8, 4, 2, 16, D), BF16),
    "acc_g": VMEM((256, HID), F32),
    "acc_u": VMEM((256, HID), F32),
    "act_s": VMEM((8, 8, 2, 8, HID), F32),
}
COPIES = {
    "a1": (4,),
    "a2": (8,),
    "b1": (4,),
    "b2": (8,),
    "d1": (16,),
    "d2": (8,),
    "l1": (16,),
    "oy": (4,),
    "os": (4,),
    "yx": (2, 4),
    "p": (16,),
    "hx": (4,),
    "ex": (4,),
    "ey": (6,),
    "zr": (2, 5, 3),
    "z4": (1,),
    "pr": (8,),
    "zs": (8, 4),
}
OPERANDS = list(LOADED) + ["out_w"]
BUFFERS = list(LOADED) + list(SCRATCH)


def mod(a, n):
    return lax.rem(a, jnp.int32(n))


def iota(shape, dim):
    return lax.broadcasted_iota(jnp.int32, shape, dim)


def silu(v):
    return v / (1.0 + jnp.exp(-v))


def kernel(*refs):
    hbm = dict(zip(OPERANDS, refs))
    refs = refs[len(OPERANDS) :]
    stream_out, state_out, act_out = refs[:3]
    refs = refs[3:]
    b = types.SimpleNamespace(**dict(zip(BUFFERS, refs)))
    refs = refs[len(BUFFERS) :]
    sems = {name: (refs[2 * n], refs[2 * n + 1]) for n, name in enumerate(COPIES)}
    loc = refs[2 * len(COPIES)]

    me = lax.axis_index("req")
    mp = lax.axis_index("mp")
    x = lax.div(me, jnp.int32(8))
    j = mod(me, 8)
    ylo = lax.div(j, jnp.int32(2))
    core = mod(me, 2)
    z = lax.div(mp, jnp.int32(2))
    hi = mod(mp, 2)
    yy = hi * 4 + ylo
    odd = mod(ylo, 2)
    pair = lax.div(yy, jnp.int32(2))
    half_of = lax.div(z, jnp.int32(4))

    def req_of(px, pylo, pcore):
        return px * 8 + pylo * 2 + pcore

    pending = []

    def send(name, at, src, dst, to_req, to_mp):
        copy = pltpu.make_async_remote_copy(
            src_ref=src,
            dst_ref=dst,
            send_sem=sems[name][0].at[at],
            recv_sem=sems[name][1].at[at],
            device_id=(to_req, to_mp),
            device_id_type=MESH,
        )
        copy.start()
        pending.append(copy)
        return copy

    loads = {}
    for n, name in enumerate(LOADED):
        loads[name] = pltpu.make_async_copy(hbm[name], getattr(b, name), loc.at[n])
        loads[name].start()
    load_o = pltpu.make_async_copy(hbm["out_w"], b.ow.at[j], loc.at[len(LOADED)])
    load_o.start()

    x_at = {d: mod(x + d, 4) for d in (1, 2, 3)}
    j_at = {d: mod(j + d, 8) for d in range(1, 8)}
    x_to = {d: req_of(x_at[d], ylo, core) for d in (1, 2, 3)}
    j_to = {d: x * 8 + j_at[d] for d in range(1, 8)}
    mp_to = {}
    for dz in range(8):
        for dh in range(2):
            if dz or dh:
                mp_to[dz * 2 + dh] = mod(z + dz, 8) * 2 + mod(hi + dh, 2)
    sibling = req_of(x, ylo, 1 - core)
    partner = req_of(x, ylo + 1 - 2 * odd, core)

    barrier = pltpu.get_barrier_semaphore()
    greet = [(x_to[d], mp) for d in x_to]
    greet += [(j_to[d], mp) for d in j_to]
    greet += [(me, mp_to[d]) for d in mp_to]
    greet += [(req_of(x, mod(ylo + d, 4), core), z * 2 + 1 - hi) for d in (1, 2, 3)]
    for to in greet:
        pl.semaphore_signal(barrier, inc=1, device_id=to, device_id_type=MESH)

    b.cc16[...] = jnp.zeros_like(b.cc16)
    loads["prefix_of"].wait()
    loads["conv_cache"].wait()
    for s in range(2):
        for k in range(3):
            for q in range(4):
                at = 4 * k + q
                b.cc16[s, at : at + 1, :] = b.conv_cache[k, s : s + 1, q * 128 : q * 128 + 128]

    def owned(t):
        p = b.prefix_of[t]
        f0 = jnp.where(p == 2 * me, 1.0, 0.0).astype(F32)
        f1 = jnp.where(p == 2 * me + 1, 1.0, 0.0).astype(F32)
        return f0, f1

    def fill_a(t, _):
        f0, f1 = owned(t)
        b.a_send[t // 8, t % 8] = (b.cc16[0] * f0 + b.cc16[1] * f1).astype(BF16)
        return 0

    lax.fori_loop(0, 32, fill_a, 0)
    pl.semaphore_wait(barrier, len(greet))

    a1 = {d: send("a1", d, b.a_send.at[x_at[d]], b.a_recv1.at[d], x_to[d], mp) for d in x_to}

    loads["xin"].wait()
    b.xpad[0:8, :] = jnp.zeros((8, CH), F32)
    b.xpad[8 : 8 + SUF, :] = b.xin[0].astype(F32)
    b.d_send[:, :, 256:384] = jnp.zeros((8, 8, 128), F32)
    for name in ("conv_w", "conv_bias", "x_proj"):
        loads[name].wait()
    rows_by_rows = (((1,), (1,)), ((), ()))

    def project_in(n):
        conv = b.conv_w[0:1, :] * b.xpad[5 : 5 + n, :]
        for k in range(1, 4):
            conv = conv + b.conv_w[k : k + 1, :] * b.xpad[5 + k : 5 + k + n, :]
        u16 = silu(conv + b.conv_bias[...]).astype(BF16)
        b.u_s[0:n, :] = u16.astype(F32)
        part = lax.dot_general(u16, b.x_proj[0:DTR, :], rows_by_rows, preferred_element_type=F32)
        part_bc = lax.dot_general(
            u16, b.x_proj[DTR : DTR + 2 * NS, :], rows_by_rows, preferred_element_type=F32
        )
        b.d_send[0 : n // 8, :, 0:DTR] = part.reshape(n // 8, 8, DTR)
        b.d_send[0 : n // 8, :, DTR : DTR + 2 * NS] = part_bc.reshape(n // 8, 8, 2 * NS)

    project_in(SUF)
    d1 = {
        rel: send("d1", rel, b.d_send.at[mod(z + rel // 2, 8)], b.d_recv.at[rel], me, mp_to[rel])
        for rel in mp_to
    }

    for d in x_to:
        a1[d].wait_recv()

    def mid_a(i, _):
        total = b.a_send[x, i].astype(F32)
        for d in (1, 2, 3):
            total = total + b.a_recv1[d, i].astype(F32)
        b.a_mid[i] = total.astype(BF16)
        return 0

    lax.fori_loop(0, 8, mid_a, 0)
    a2 = {d: send("a2", d, b.a_mid.at[j_at[d]], b.a_recv2.at[d], j_to[d], mp) for d in j_to}

    oy = {}
    for d in (1, 2, 3):
        to = req_of(x, mod(ylo + d, 4), core)
        oy[d] = send("oy", d, hbm["out_w"], b.ow.at[j], to, mp)
    osib = {0: send("os", 0, hbm["out_w"], b.ow.at[j], sibling, mp)}

    loads["ids"].wait()
    loads["gate_w"].wait()
    eye = iota((SUF, SUF), 0) == iota((SUF, SUF), 1)

    def column(row):
        return jnp.sum(jnp.where(eye, row, 0.0), axis=1, keepdims=True)

    id_rows = b.ids[...].astype(F32)
    gate_rows = b.gate_w[...].astype(F32)
    ids = [column(id_rows[k : k + 1, :]) for k in range(2)]
    gates = [column(gate_rows[k : k + 1, :]) for k in range(2)]
    lane8 = iota((SUF, 128), 1).astype(F32)
    onehot = (
        jnp.where(ids[0] == lane8, 1.0, 0.0) + jnp.where(ids[1] == lane8, 1.0, 0.0)
    ).astype(BF16)
    tri_r, tri_c = iota((SUF, 1), 0), iota((1, SUF), 1)
    tri = jnp.where((tri_r // 4 == tri_c // 4) & (tri_c < tri_r), 1.0, 0.0).astype(BF16)
    before = jnp.dot(tri, onehot, preferred_element_type=F32)
    ranks = [
        jnp.sum(jnp.where(ids[k] == lane8, before, 0.0), axis=1, keepdims=True) for k in range(2)
    ]
    lane = iota((1, 128), 1)
    lane_block = jnp.where((lane % 64 < 32) & (lane // 64 == core), (lane % 64) // 2, -1)
    place = iota((SUF, 1), 0) // 4 == lane_block
    lane_rank = (lane % 2).astype(F32)
    row16 = iota((16, 128), 0)

    def fill_g(e, _):
        total = jnp.zeros((1, 128), F32)
        for k in range(2):
            hit = place & (ids[k] == e.astype(F32)) & (ranks[k] == lane_rank)
            total = total + jnp.sum(jnp.where(hit, gates[k], 0.0), axis=0, keepdims=True)
        b.gmat[e] = jnp.where(
            row16 == lax.div(me, jnp.int32(2)), jnp.broadcast_to(total, (16, 128)), 0.0
        ).astype(BF16)
        return 0

    lax.fori_loop(0, EXPERTS, fill_g, 0)

    for rel in mp_to:
        d1[rel].wait_recv()
    total = b.d_send[z]
    for rel in mp_to:
        total = total + b.d_recv[rel]
    b.d_sum[...] = total
    b.d_all[z] = total
    d2 = {
        dz: send("d2", dz, b.d_sum, b.d_all.at[z], me, mod(z + dz, 8) * 2 + hi)
        for dz in range(1, 8)
    }

    for d in j_to:
        a2[d].wait_recv()
    total = b.a_mid[j].astype(F32)
    for d in j_to:
        total = total + b.a_recv2[d].astype(F32)
    b.cs16[...] = total
    for k in range(3):
        for q in range(4):
            at = 4 * k + q
            b.xpad[5 + k : 6 + k, q * 128 : q * 128 + 128] = b.cs16[at : at + 1, :]
    for rel in mp_to:
        d1[rel].wait_send()
    pending[:] = [c for c in pending if not any(c is d1[rel] for rel in d1)]
    project_in(16)
    tail = b.d_send[0, :, 256:384]
    b.l_send[...] = jnp.zeros((8, 128), F32)
    for t in range(3):
        b.l_send[2 * t : 2 * t + 1, :] = b.d_send[0, t : t + 1, 0:128]
        b.l_send[2 * t + 1 : 2 * t + 2, :] = b.d_send[0, t : t + 1, 128:256]
    b.l_send[6:7, :] = (
        tail[0:1, :] + pltpu.roll(tail, 32, 1)[1:2, :] + pltpu.roll(tail, 64, 1)[2:3, :]
    )
    l1 = {
        rel: send("l1", rel, b.l_send, b.l_recv.at[rel], me, mp_to[rel]) for rel in mp_to
    }

    loads["ssm_cache"].wait()

    def fill_b(t, _):
        f0, f1 = owned(t)
        px, at = lax.div(t, jnp.int32(8)), mod(t, 8)
        b.b_send[px, at, :, 0:CH] = (b.ssm_cache[0] * f0 + b.ssm_cache[1] * f1).astype(BF16)
        b.b_send[px, at, :, CH : CH + 128] = b.gmat[lax.div(t, jnp.int32(4))]
        return 0

    lax.fori_loop(0, 32, fill_b, 0)
    b1 = {d: send("b1", d, b.b_send.at[x_at[d]], b.b_recv1.at[d], x_to[d], mp) for d in x_to}

    for name in ("dt_proj", "dt_bias", "a_log", "d_skip", "zin"):
        loads[name].wait()
    for dz in d2:
        d2[dz].wait_recv()
    mask_b = jnp.where(iota((NS, 128), 1) == iota((NS, 128), 0), 1.0, 0.0)
    mask_c = jnp.where(iota((NS, 128), 1) == iota((NS, 128), 0) + NS, 1.0, 0.0)

    def steps(n):
        dbc_in = b.d_all[0 : n // 8, :, 0:DTR].reshape(n, DTR).astype(BF16)
        pre = jnp.dot(dbc_in, b.dt_proj[...], preferred_element_type=F32) + b.dt_bias[...]
        b.dt_s[0:n, :] = jnp.maximum(pre, 0.0) + jnp.log1p(jnp.exp(-jnp.abs(pre)))

    def spread(i, _):
        rows = b.d_all[i, :, DTR : DTR + 128]
        for t in range(8):
            one = jnp.broadcast_to(rows[t : t + 1, :], (NS, 128))
            b.b_exp[i * 8 + t] = jnp.broadcast_to(
                jnp.sum(one * mask_b, axis=1, keepdims=True), (NS, 128)
            )
            b.c_exp[i * 8 + t] = jnp.broadcast_to(
                jnp.sum(one * mask_c, axis=1, keepdims=True), (NS, 128)
            )
        return 0

    steps(SUF)
    lax.fori_loop(1, 8, spread, 0)

    for d in x_to:
        b1[d].wait_recv()

    def mid_b(i, _):
        total = b.b_send[x, i].astype(F32)
        for d in (1, 2, 3):
            total = total + b.b_recv1[d, i].astype(F32)
        b.b_mid[i] = total.astype(BF16)
        return 0

    lax.fori_loop(0, 8, mid_b, 0)
    b2 = {d: send("b2", d, b.b_mid.at[j_at[d]], b.b_recv2.at[d], j_to[d], mp) for d in j_to}

    for rel in mp_to:
        l1[rel].wait_recv()
    total = b.l_send[...]
    for rel in mp_to:
        total = total + b.l_recv[rel]
    last = jnp.broadcast_to(total[6:7, :], (8, 128))
    for t in range(3):
        b.d_all[0, t : t + 1, 0:128] = total[2 * t : 2 * t + 1, :]
        b.d_all[0, t : t + 1, 128:256] = total[2 * t + 1 : 2 * t + 2, :]
        moved = pltpu.roll(last, 128 - 32 * t, 1) if t else last
        b.d_all[0, t : t + 1, 256:384] = moved[0:1, :]
    steps(16)
    spread(0, 0)

    for d in (1, 2, 3):
        oy[d].wait_recv()
        block = b.ow.at[mod(ylo + 4 - d, 4) * 2 + core]
        osib[d] = send("os", d, block, block, sibling, mp)

    row = iota((128, 1), 0)
    wide = iota((128, 128), 1)
    target = ((row // 4) % 4) * 32 + (row // 16) * 4 + row % 4
    b.perm_rows[...] = jnp.where(wide == target, 1.0, 0.0).astype(BF16)
    target = (row % 16) * 8 + row // 16
    b.perm_small[...] = jnp.where(wide == target, 1.0, 0.0).astype(BF16)
    target = ((row % 32) // 2) * 8 + (row // 32) * 2 + row % 2
    b.perm_out[...] = jnp.where(wide == target, 1.0, 0.0).astype(BF16)
    col = iota((1, 32), 1)
    mine = iota((SUF, 1), 0) == mp * 4 + (col // 2) % 4
    col_group = (col // 8) * 2 + col % 2
    chosen = jnp.zeros((128, 32), F32)
    for k in range(2):
        id_row = jnp.sum(jnp.where(mine, ids[k], 0.0), axis=0, keepdims=True)
        rank_row = jnp.sum(jnp.where(mine, ranks[k], 0.0), axis=0, keepdims=True)
        hit = (
            (row % 8 == col_group)
            & ((row // 16).astype(F32) == id_row)
            & (((row // 8) % 2).astype(F32) == rank_row)
        )
        chosen = chosen + jnp.where(hit, 1.0, 0.0)
    b.sel[...] = chosen.astype(BF16)
    loads["resid"].wait()
    loads["norm_gain"].wait()
    b.r4[...] = b.resid[...].astype(F32)
    for q in range(8):
        for part_ in range(4):
            at = q * 4 + part_
            b.g8[q : q + 1, part_ * 128 : part_ * 128 + 128] = b.norm_gain[at : at + 1, :]
    for px in range(4):
        for t in range(4):
            for half in range(2):
                at, q = t * 2 + half, px * 2 + half
                b.r32[px, at : at + 1, :] = b.r4[t : t + 1, q * 512 : q * 512 + 512]
                b.g32[px, at : at + 1, :] = b.g8[q : q + 1, :]

    for d in j_to:
        b2[d].wait_recv()
    total = b.b_mid[j].astype(F32)
    for d in j_to:
        total = total + b.b_recv2[d].astype(F32)
    gates16 = total[:, CH : CH + 128].astype(BF16)
    amat = -jnp.exp(b.a_log[...])

    def widen(v):
        return jnp.concatenate([v, v, v, v], axis=1)

    def scan8(i, state):
        at = pl.ds(pl.multiple_of(i * 8, 8), 8)
        dt8 = b.dt_s[at, :]
        du8 = dt8 * b.u_s[at, :]
        for t in range(8):
            decay = jnp.exp(dt8[t : t + 1, :] * amat)
            state = decay * state + widen(b.b_exp[i * 8 + t]) * du8[t : t + 1, :]
            b.yv_s[pl.ds(i * 8 + t, 1), :] = jnp.sum(
                widen(b.c_exp[i * 8 + t]) * state, axis=0, keepdims=True
            )
        return state

    yx = {}

    def mixed(half, state):
        state = lax.fori_loop(4 * half, 4 * half + 4, scan8, state)
        at = slice(32 * half, 32 * half + 32)
        gated = (b.yv_s[at, :] + b.d_skip[...] * b.u_s[at, :]) * silu(b.zin[0, at, :].astype(F32))
        ymix = gated.astype(BF16)
        b.ymix[half] = ymix
        b.yfull[half, x] = ymix
        for d in x_to:
            yx[half, d] = send(
                "yx", (half, d), b.ymix.at[half], b.yfull.at[half, x], x_to[d], mp
            )
        return state

    index = mod(mp, 8)

    def project_out(half):
        for d in x_to:
            yx[half, d].wait_recv()
        left = jnp.dot(
            b.perm_rows[...], b.yfull[half].reshape(128, CH), preferred_element_type=F32
        ).astype(BF16)
        for n in range(4):
            cols = jnp.concatenate([b.ow[2 * n], b.ow[2 * n + 1]], axis=1)
            part = jnp.dot(left, cols, preferred_element_type=F32).astype(BF16)
            b.p_send[8 * half : 8 * half + 8, :, n * 256 : n * 256 + 256] = part.reshape(
                8, 16, 256
            )
        apart = half + half_of - 2 * half * half_of
        for d in range(1, 8):
            to = 8 * half + mod(index + d, 8)
            slot = 8 * apart + d
            send("p", slot, b.p_send.at[to], b.p_recv.at[slot], me, to)

    state = mixed(0, total[:, 0:CH])
    state = mixed(1, state)
    load_o.wait()
    for d in osib:
        osib[d].wait_recv()
    project_out(0)
    project_out(1)
    across = mod(mp + 8, 16)
    send("p", 8, b.p_send.at[across], b.p_recv.at[8], me, across)
    state_out[...] = state
    total = b.p_send[mp].astype(F32)
    for slot in range(1, 16):
        pltpu.make_async_remote_copy(
            src_ref=b.p_send.at[0],
            dst_ref=b.p_recv.at[slot],
            send_sem=sems["p"][0].at[slot],
            recv_sem=sems["p"][1].at[slot],
            device_id=(me, mp),
            device_id_type=MESH,
        ).wait_recv()
        total = total + b.p_recv[slot].astype(F32)
    b.p_sum[...] = total
    for px in range(4):
        for t in range(4):
            for half in range(2):
                at = t * 2 + half
                b.hx_send[px, at : at + 1, :] = b.p_sum[
                    px * 4 + t : px * 4 + t + 1, half * 512 : half * 512 + 512
                ]
    hx = {d: send("hx", d, b.hx_send.at[x_at[d]], b.hx_recv.at[x], x_to[d], mp) for d in x_to}
    b.hx_recv[x] = b.hx_send[x]
    for d in x_to:
        hx[d].wait_recv()

    hidden = [b.hx_recv[px] + b.r32[px] for px in range(4)]
    square = hidden[0] * hidden[0]
    for px in range(1, 4):
        square = square + hidden[px] * hidden[px]
    square = jnp.sum(square, axis=1, keepdims=True)
    scales = []
    for t in range(4):
        mean = (square[2 * t : 2 * t + 1] + square[2 * t + 1 : 2 * t + 2]) * (1.0 / D)
        scales += [lax.rsqrt(mean + 1e-05)] * 2
    scale = jnp.concatenate([jnp.broadcast_to(v, (1, 512)) for v in scales], axis=0)
    normed = [hidden[px] * scale * b.g32[px] for px in range(4)]
    b.n32[...] = jnp.concatenate(normed, axis=0).astype(BF16)
    b.e_send[...] = (
        jnp.dot(b.sel[...], b.n32[...], preferred_element_type=F32)
        .astype(BF16)
        .reshape(EXPERTS, 16, 512)
    )

    ex = {
        d: send(
            "ex", d, b.e_send.at[pl.ds(2 * x_at[d], 2)], b.e_mid.at[:, x], x_to[d], mp
        )
        for d in x_to
    }
    b.e_mid[0, x] = b.e_send[2 * x]
    b.e_mid[1, x] = b.e_send[2 * x + 1]
    for px in range(4):
        for t in range(4):
            for half in range(2):
                at, q = t * 2 + half, px * 2 + half
                b.h4[t : t + 1, q * 512 : q * 512 + 512] = hidden[px][at : at + 1, :]
    stream_out[...] = b.h4[...].astype(BF16)
    for d in x_to:
        ex[d].wait_recv()

    kind = mod(pair, 2)

    def send_y(slot, to_y, parity):
        return send(
            "ey",
            slot * 2 + odd,
            b.e_mid.at[parity],
            b.e_recv.at[slot, odd],
            req_of(x, mod(to_y, 4), core),
            z * 2 + lax.div(to_y, jnp.int32(4)),
        )

    send_y(0, yy + 1 - 2 * odd, kind)
    send_y(1, 2 * mod(pair + 1, 4), 1 - kind)
    send_y(1, 2 * mod(pair + 3, 4) + 1, 1 - kind)
    send_y(2, 2 * mod(pair + 2, 4), kind)
    send_y(2, 2 * mod(pair + 2, 4) + 1, kind)
    b.e_recv[0, odd] = b.e_mid[kind]

    def got_y(slot, member):
        pltpu.make_async_remote_copy(
            src_ref=b.e_mid.at[0],
            dst_ref=b.e_recv.at[slot, member],
            send_sem=sems["ey"][0].at[slot * 2 + member],
            recv_sem=sems["ey"][1].at[slot * 2 + member],
            device_id=(me, mp),
            device_id_type=MESH,
        ).wait_recv()

    own_side = 3 - 2 * odd
    chunk = (0, own_side, 2)

    def ring(way, s, i):
        if way == 0:
            block, to = mod(z + 9 - s, 8), mod(z + 1, 8)
        else:
            block, to = mod(z + s - 1, 8), mod(z + 7, 8)
        ref = b.xb.at[block, chunk[i], core]
        return send("zr", (way, s, i), ref, ref, me, to * 2 + hi)

    def in_ring(way, s, i):
        return s <= 3 or (s == 4 and i == way)

    def share(row, block, i):
        ref = b.xb.at[block, chunk[i] if i < 3 else 4 - own_side, core]
        return send("zs", (row, i), ref, ref, sibling, mp)

    def to_pair(row, block):
        ref = b.xb.at[block, own_side, core]
        return send("pr", row, ref, ref, partner, mp)

    block_of = {0: z, 7: mod(z + 4, 8)}
    for s in (1, 2, 3):
        block_of[2 * s - 1] = mod(z + 8 - s, 8)
        block_of[2 * s] = mod(z + s, 8)

    zr, zs, pr = {}, {}, {}
    for i in range(3):
        if i == 0:
            got_y(0, 1 - odd)
        else:
            got_y(i, 0)
            got_y(i, 1)
        raw = b.e_recv[i].reshape(128, 512)
        rows = jnp.dot(b.perm_small[...], raw, preferred_element_type=F32).astype(BF16)
        for q in range(8):
            b.xb[z, chunk[i], core, :, q * 512 : q * 512 + 512] = rows[q * 16 : q * 16 + 16, :]
        zr[0, 1, i] = ring(0, 1, i)
        zr[1, 1, i] = ring(1, 1, i)
        zs[0, i] = share(0, z, i)
        if i == 1:
            pr[0] = to_pair(0, z)

    def handle(s, i):
        for way in (0, 1):
            if (way, s, i) not in zr:
                continue
            zr[way, s, i].wait_recv()
            if in_ring(way, s + 1, i):
                zr[way, s + 1, i] = ring(way, s + 1, i)
            row = 2 * s - 1 + way if s < 4 else 7
            zs[row, i] = share(row, block_of[row], i)
            if i == 1:
                pr[row] = to_pair(row, block_of[row])

    def from_pair(rows):
        for row in rows:
            pr[row].wait_recv()
            zs[row, 3] = share(row, block_of[row], 3)

    i_row = iota((128, 1), 0)
    grp, cc, yi, xs, kk = (
        i_row // 32,
        (i_row // 16) % 2,
        (i_row // 8) % 2,
        (i_row // 2) % 4,
        i_row % 2,
    )
    source = (2 * pair + 2 * grp + yi) % 8
    pick = jnp.where(iota((128, 16), 1) == xs * 4 + source % 4, 1.0, 0.0).astype(BF16)
    spread_g = jnp.dot(pick, gates16, preferred_element_type=F32)
    gate_lane = cc * 64 + (source // 4) * 2 + kk

    def expert(rows):
        for row in rows:
            for i in range(4):
                zs[row, i].wait_recv()
        blocks = [block_of[row] for row in rows]
        m = 128 * len(blocks)
        b.acc_g[0:m, :] = jnp.zeros((m, HID), F32)
        b.acc_u[0:m, :] = jnp.zeros((m, HID), F32)

        def tile(k, _):
            ks = pl.ds(pl.multiple_of(k * KT, KT), KT)
            slots = jnp.concatenate(
                [b.xb[block, :, :, :, ks].reshape(128, KT) for block in blocks], axis=0
            )
            b.acc_g[0:m, :] += jnp.dot(slots, b.w_gate[0, ks, :], preferred_element_type=F32)
            b.acc_u[0:m, :] += jnp.dot(slots, b.w_up[0, ks, :], preferred_element_type=F32)
            return 0

        lax.fori_loop(0, D // KT, tile, 0)
        for n, block in enumerate(blocks):
            here = iota((128, 128), 1) == gate_lane + block * 4
            weight = jnp.sum(jnp.where(here, spread_g, 0.0), axis=1, keepdims=True)
            part = slice(n * 128, n * 128 + 128)
            act = silu(b.acc_g[part, :]) * b.acc_u[part, :] * weight
            for g in range(4):
                for c in range(2):
                    for member in range(2):
                        at = g * 32 + c * 16 + member * 8
                        b.act_s[block, mod(2 * pair + 2 * g + member, 8), c] = act[at : at + 8, :]

    loads["w_gate"].wait()
    loads["w_up"].wait()
    for s in (1, 2, 3):
        for i in range(3):
            handle(s, i)
        if s == 3:
            ref = b.xb.at[mod(z + 5 + core * 6, 8), 2, core]
            z4 = send("z4", 0, ref, ref, me, mod(z + 1 + core * 6, 8) * 2 + hi)
        from_pair([0] if s == 1 else [2 * s - 3, 2 * s - 2])
        if s == 2:
            expert([0])
        if s == 3:
            expert([1, 2])
    handle(4, 0)
    handle(4, 1)
    from_pair([5, 6])
    expert([3, 4])
    z4.wait_recv()
    zs[7, 2] = share(7, block_of[7], 2)
    expert([5, 6])
    from_pair([7])
    expert([7])

    for line in range(4):
        for c in range(2):
            rows = jnp.concatenate(
                [b.act_s[pz, ph * 4 + line, c] for pz in range(8) for ph in range(2)], axis=0
            ).astype(BF16)
            rows = jnp.dot(b.perm_out[...], rows, preferred_element_type=F32).astype(BF16)
            for px in range(4):
                at = ((px * 4 + line) * 2 + c) * 32
                act_out[at : at + 32, :] = rows[px * 32 : px * 32 + 32, :]

    for copy in pending:
        copy.wait_send()


def local(
    xin,
    zin,
    conv_w,
    conv_bias,
    x_proj,
    dt_proj,
    dt_bias,
    a_log,
    d_skip,
    conv_cache,
    ssm_cache,
    prefix_of,
    out_w,
    resid,
    norm_gain,
    expert_ids,
    gate_w,
    w_gate,
    w_up,
):
    operands = {
        "prefix_of": prefix_of,
        "conv_cache": conv_cache.transpose(1, 0, 2),
        "ids": expert_ids.T,
        "gate_w": gate_w.T,
        "ssm_cache": ssm_cache,
        "xin": xin,
        "conv_w": conv_w,
        "conv_bias": conv_bias.reshape(1, CH),
        "x_proj": x_proj.T,
        "resid": resid,
        "norm_gain": norm_gain.reshape(32, 128),
        "dt_proj": dt_proj,
        "dt_bias": dt_bias.reshape(1, CH),
        "a_log": a_log,
        "d_skip": d_skip.reshape(1, CH),
        "zin": zin,
        "w_gate": w_gate,
        "w_up": w_up,
        "out_w": out_w,
    }
    vmem = pl.BlockSpec(memory_space=VMEM)
    dma = pltpu.SemaphoreType.DMA
    sems = []
    for shape in COPIES.values():
        sems += [dma(shape), dma(shape)]
    sems.append(dma((len(LOADED) + 1,)))
    stream, state, act = pl.pallas_call(
        kernel,
        out_shape=(
            jax.ShapeDtypeStruct((4, D), BF16),
            jax.ShapeDtypeStruct((NS, CH), F32),
            jax.ShapeDtypeStruct((1024, HID), BF16),
        ),
        in_specs=[pl.BlockSpec(memory_space=pltpu.HBM)] * len(OPERANDS),
        out_specs=(vmem, vmem, vmem),
        scratch_shapes=list(LOADED.values()) + list(SCRATCH.values()) + sems,
        compiler_params=pltpu.CompilerParams(
            collective_id=0, has_side_effects=True, vmem_limit_bytes=60 * 1024 * 1024
        ),
        name="mixer_and_experts",
    )(*[operands[name] for name in OPERANDS])
    return (stream, state[None], act[None])


def solution(mesh):
    placed = (
        P("req", None, "mp"),
        P("req", None, "mp"),
        P(None, "mp"),
        P("mp"),
        P("mp", None),
        P(None, "mp"),
        P("mp"),
        P(None, "mp"),
        P("mp"),
        P("req", None, "mp"),
        P("req", None, "mp"),
        P(),
        P("mp", "req"),
        P(("req", "mp"), None),
        P(),
        P("req", None),
        P("req", None),
        P("req", None, "mp"),
        P("req", None, "mp"),
    )
    return jax.shard_map(
        local,
        mesh=mesh,
        in_specs=placed,
        out_specs=(P(("req", "mp"), None), P("req", None, "mp"), P("req", None, "mp")),
        check_vma=False,
    )
```

```python
import types

import jax
import jax.numpy as jnp
from jax import lax
from jax.experimental import pallas as pl
from jax.experimental.pallas import tpu as pltpu
from jax.sharding import PartitionSpec as P

F32 = jnp.float32
BF16 = jnp.bfloat16
MESH = pl.DeviceIdType.MESH

D = 4096
CH = 512
NS = 16
SUF = 64
DTR = 256
EXPERTS = 8
HID = 256
KT = 1024

VMEM = pltpu.VMEM
LOADED = {
    "prefix_of": pltpu.SMEM((32,), jnp.int32),
    "conv_cache": VMEM((3, 2, CH), F32),
    "ids": VMEM((2, SUF), jnp.int32),
    "gate_w": VMEM((2, SUF), BF16),
    "ssm_cache": VMEM((2, NS, CH), F32),
    "xin": VMEM((1, SUF, CH), BF16),
    "conv_w": VMEM((4, CH), F32),
    "conv_bias": VMEM((1, CH), F32),
    "x_proj": VMEM((DTR + 2 * NS, CH), BF16),
    "resid": VMEM((4, D), BF16),
    "norm_gain": VMEM((32, 128), F32),
    "dt_proj": VMEM((DTR, CH), BF16),
    "dt_bias": VMEM((1, CH), F32),
    "a_log": VMEM((NS, CH), F32),
    "d_skip": VMEM((1, CH), F32),
    "zin": VMEM((1, SUF, CH), BF16),
    "w_gate": VMEM((1, D, HID), BF16),
    "w_up": VMEM((1, D, HID), BF16),
}
SCRATCH = {
    "cc16": VMEM((2, 16, 128), F32),
    "cs16": VMEM((16, 128), F32),
    "xpad": VMEM((72, CH), F32),
    "c_send": VMEM((2, 16, CH + 128), BF16),
    "c_recv": VMEM((4, 2, 16, CH + 128), BF16),
    "g_recv": VMEM((4, 2, 16, 128), BF16),
    "a_mid": VMEM((8, 16, 128), BF16),
    "a_recv2": VMEM((8, 16, 128), BF16),
    "b_mid": VMEM((8, 16, CH + 128), BF16),
    "b_recv2": VMEM((8, 16, CH + 128), BF16),
    "gmat": VMEM((8, 16, 128), BF16),
    "d_send": VMEM((8, 8, 384), F32),
    "d_recv": VMEM((8, 8, 384), F32),
    "d_part": VMEM((8, 384), F32),
    "d_other": VMEM((8, 384), F32),
    "d_sum": VMEM((8, 384), F32),
    "d_all": VMEM((8, 8, 384), F32),
    "l_send": VMEM((8, 128), F32),
    "l_recv": VMEM((16, 8, 128), F32),
    "dt_s": VMEM((SUF, CH), F32),
    "u_s": VMEM((SUF, CH), F32),
    "yv_s": VMEM((SUF, CH), F32),
    "b_exp": VMEM((SUF, NS, 128), F32),
    "c_exp": VMEM((SUF, NS, 128), F32),
    "ow": VMEM((8, CH, 128), BF16),
    "ymix": VMEM((2, 32, CH), BF16),
    "yfull": VMEM((2, 4, 32, CH), BF16),
    "perm_rows": VMEM((128, 128), BF16),
    "perm_out": VMEM((128, 128), BF16),
    "perm_small": VMEM((128, 128), BF16),
    "p_send": VMEM((16, 16, 1024), BF16),
    "p_recv": VMEM((8, 2, 16, 1024), BF16),
    "p_relay": VMEM((2, 16, 1024), BF16),
    "p_part": VMEM((16, 1024), BF16),
    "p_other": VMEM((16, 1024), BF16),
    "p_sum": VMEM((16, 1024), F32),
    "hx_send": VMEM((4, 8, 512), F32),
    "hx_recv": VMEM((4, 8, 512), F32),
    "r4": VMEM((4, D), F32),
    "r32": VMEM((4, 8, 512), F32),
    "g8": VMEM((8, 512), F32),
    "g32": VMEM((4, 8, 512), F32),
    "n32": VMEM((32, 512), BF16),
    "h4": VMEM((4, D), F32),
    "sel": VMEM((128, 32), BF16),
    "e_send": VMEM((8, 16, 512), BF16),
    "e_mid": VMEM((2, 4, 16, 512), BF16),
    "e_recv": VMEM((3, 2, 4, 16, 512), BF16),
    "xb": VMEM((8, 4, 2, 16, D), BF16),
    "acc_g": VMEM((256, HID), F32),
    "acc_u": VMEM((256, HID), F32),
    "act_s": VMEM((8, 8, 2, 8, HID), F32),
}
COPIES = {
    "c1": (4,),
    "g1": (4,),
    "a2": (8,),
    "b2": (8,),
    "d1": (8,),
    "dy": (1,),
    "d2": (8,),
    "l1": (16,),
    "oy": (4,),
    "os": (4,),
    "yx": (2, 4),
    "p": (8,),
    "py": (1,),
    "hx": (4,),
    "ex": (4,),
    "ey": (6,),
    "zr": (2, 5, 3),
    "z4": (1,),
    "pr": (8,),
    "zs": (8, 4),
}
OPERANDS = list(LOADED) + ["out_w"]
BUFFERS = list(LOADED) + list(SCRATCH)


def mod(a, n):
    return lax.rem(a, jnp.int32(n))


def iota(shape, dim):
    return lax.broadcasted_iota(jnp.int32, shape, dim)


def silu(v):
    return v / (1.0 + jnp.exp(-v))


def kernel(*refs):
    hbm = dict(zip(OPERANDS, refs))
    refs = refs[len(OPERANDS) :]
    stream_out, state_out, act_out = refs[:3]
    refs = refs[3:]
    b = types.SimpleNamespace(**dict(zip(BUFFERS, refs)))
    refs = refs[len(BUFFERS) :]
    sems = {name: (refs[2 * n], refs[2 * n + 1]) for n, name in enumerate(COPIES)}
    loc = refs[2 * len(COPIES)]

    me = lax.axis_index("req")
    mp = lax.axis_index("mp")
    x = lax.div(me, jnp.int32(8))
    j = mod(me, 8)
    ylo = lax.div(j, jnp.int32(2))
    core = mod(me, 2)
    z = lax.div(mp, jnp.int32(2))
    hi = mod(mp, 2)
    yy = hi * 4 + ylo
    odd = mod(ylo, 2)
    pair = lax.div(yy, jnp.int32(2))
    z_at = {dz: mod(z + dz, 8) for dz in range(1, 8)}
    over_y = z * 2 + 1 - hi

    def req_of(px, pylo, pcore):
        return px * 8 + pylo * 2 + pcore

    pending = []

    def send(name, at, src, dst, to_req, to_mp):
        copy = pltpu.make_async_remote_copy(
            src_ref=src,
            dst_ref=dst,
            send_sem=sems[name][0].at[at],
            recv_sem=sems[name][1].at[at],
            device_id=(to_req, to_mp),
            device_id_type=MESH,
        )
        copy.start()
        pending.append(copy)
        return copy

    loads = {}
    for n, name in enumerate(LOADED):
        loads[name] = pltpu.make_async_copy(hbm[name], getattr(b, name), loc.at[n])
        loads[name].start()
    load_o = pltpu.make_async_copy(hbm["out_w"], b.ow.at[j], loc.at[len(LOADED)])
    load_o.start()

    x_at = {d: mod(x + d, 4) for d in (1, 2, 3)}
    j_at = {d: mod(j + d, 8) for d in range(1, 8)}
    x_to = {d: req_of(x_at[d], ylo, core) for d in (1, 2, 3)}
    j_to = {d: x * 8 + j_at[d] for d in range(1, 8)}
    mp_to = {}
    for dz in range(8):
        for dh in range(2):
            if dz or dh:
                mp_to[dz * 2 + dh] = mod(z + dz, 8) * 2 + mod(hi + dh, 2)
    sibling = req_of(x, ylo, 1 - core)
    partner = req_of(x, ylo + 1 - 2 * odd, core)

    barrier = pltpu.get_barrier_semaphore()
    greet = [(x_to[d], mp) for d in x_to]
    greet += [(j_to[d], mp) for d in j_to]
    greet += [(me, mp_to[d]) for d in mp_to]
    greet += [(req_of(x, mod(ylo + d, 4), core), z * 2 + 1 - hi) for d in (1, 2, 3)]
    for to in greet:
        pl.semaphore_signal(barrier, inc=1, device_id=to, device_id_type=MESH)

    b.cc16[...] = jnp.zeros_like(b.cc16)
    loads["prefix_of"].wait()
    loads["conv_cache"].wait()
    for s in range(2):
        for k in range(3):
            for q in range(4):
                at = 4 * k + q
                b.cc16[s, at : at + 1, :] = b.conv_cache[k, s : s + 1, q * 128 : q * 128 + 128]

    loads["ssm_cache"].wait()
    for s in range(2):
        b.c_send[s, :, 0:CH] = b.ssm_cache[s].astype(BF16)
        b.c_send[s, :, CH : CH + 128] = b.cc16[s].astype(BF16)
    b.c_recv[0] = b.c_send[...]

    loads["ids"].wait()
    loads["gate_w"].wait()
    eye = iota((SUF, SUF), 0) == iota((SUF, SUF), 1)

    def column(row):
        return jnp.sum(jnp.where(eye, row, 0.0), axis=1, keepdims=True)

    id_rows = b.ids[...].astype(F32)
    gate_rows = b.gate_w[...].astype(F32)
    ids = [column(id_rows[k : k + 1, :]) for k in range(2)]
    gates = [column(gate_rows[k : k + 1, :]) for k in range(2)]
    lane8 = iota((SUF, 128), 1).astype(F32)
    onehot = (
        jnp.where(ids[0] == lane8, 1.0, 0.0) + jnp.where(ids[1] == lane8, 1.0, 0.0)
    ).astype(BF16)
    tri_r, tri_c = iota((SUF, 1), 0), iota((1, SUF), 1)
    tri = jnp.where((tri_r // 4 == tri_c // 4) & (tri_c < tri_r), 1.0, 0.0).astype(BF16)
    before = jnp.dot(tri, onehot, preferred_element_type=F32)
    ranks = [
        jnp.sum(jnp.where(ids[k] == lane8, before, 0.0), axis=1, keepdims=True) for k in range(2)
    ]
    lane = iota((1, 128), 1)
    lane_block = jnp.where((lane % 64 < 32) & (lane // 64 == core), (lane % 64) // 2, -1)
    place = iota((SUF, 1), 0) // 4 == lane_block
    lane_rank = (lane % 2).astype(F32)
    row16 = iota((16, 128), 0)

    def fill_g(e, _):
        total = jnp.zeros((1, 128), F32)
        for k in range(2):
            hit = place & (ids[k] == e.astype(F32)) & (ranks[k] == lane_rank)
            total = total + jnp.sum(jnp.where(hit, gates[k], 0.0), axis=0, keepdims=True)
        b.gmat[e] = jnp.where(
            row16 == lax.div(me, jnp.int32(2)), jnp.broadcast_to(total, (16, 128)), 0.0
        ).astype(BF16)
        return 0

    lax.fori_loop(0, EXPERTS, fill_g, 0)

    b.g_recv[0, 0] = b.gmat[2 * x]
    b.g_recv[0, 1] = b.gmat[2 * x + 1]

    loads["xin"].wait()
    b.xpad[0:8, :] = jnp.zeros((8, CH), F32)
    b.xpad[8 : 8 + SUF, :] = b.xin[0].astype(F32)
    b.d_send[:, :, 256:384] = jnp.zeros((8, 8, 128), F32)
    for name in ("conv_w", "conv_bias", "x_proj"):
        loads[name].wait()
    rows_by_rows = (((1,), (1,)), ((), ()))

    def project_in(n):
        conv = b.conv_w[0:1, :] * b.xpad[5 : 5 + n, :]
        for k in range(1, 4):
            conv = conv + b.conv_w[k : k + 1, :] * b.xpad[5 + k : 5 + k + n, :]
        u16 = silu(conv + b.conv_bias[...]).astype(BF16)
        b.u_s[0:n, :] = u16.astype(F32)
        part = lax.dot_general(u16, b.x_proj[0:DTR, :], rows_by_rows, preferred_element_type=F32)
        part_bc = lax.dot_general(
            u16, b.x_proj[DTR : DTR + 2 * NS, :], rows_by_rows, preferred_element_type=F32
        )
        b.d_send[0 : n // 8, :, 0:DTR] = part.reshape(n // 8, 8, DTR)
        b.d_send[0 : n // 8, :, DTR : DTR + 2 * NS] = part_bc.reshape(n // 8, 8, 2 * NS)

    project_in(SUF)
    pl.semaphore_wait(barrier, len(greet))
    c1 = {d: send("c1", d, b.c_send, b.c_recv.at[d], x_to[d], mp) for d in x_to}
    d1 = {
        dz: send("d1", dz, b.d_send.at[z_at[dz]], b.d_recv.at[dz], me, z_at[dz] * 2 + hi)
        for dz in z_at
    }
    g1 = {
        d: send("g1", d, b.gmat.at[pl.ds(2 * x_at[d], 2)], b.g_recv.at[d], x_to[d], mp)
        for d in x_to
    }

    across_y = mod(ylo + 2, 4)
    beside_y = ylo + 1 - 2 * odd
    oy = {
        1: send("oy", 1, hbm["out_w"], b.ow.at[j], req_of(x, across_y, core), mp),
        2: send("oy", 2, hbm["out_w"], b.ow.at[j], partner, mp),
    }
    osib = {0: send("os", 0, hbm["out_w"], b.ow.at[j], sibling, mp)}

    for d in x_to:
        c1[d].wait_recv()

    def chosen_prefix(i, lanes):
        p = b.prefix_of[x * 8 + i]
        total = jnp.zeros((16, lanes.stop - lanes.start), F32)
        for d in range(4):
            owner = mod(x + 4 - d, 4) * 8 + j
            for s in range(2):
                here = jnp.where(p == 2 * owner + s, 1.0, 0.0).astype(F32)
                total = total + b.c_recv[d, s, :, lanes].astype(F32) * here
        return total.astype(BF16)

    def mid_a(i, _):
        b.a_mid[i] = chosen_prefix(i, slice(CH, CH + 128))
        return 0

    lax.fori_loop(0, 8, mid_a, 0)
    a2 = {d: send("a2", d, b.a_mid.at[j_at[d]], b.a_recv2.at[d], j_to[d], mp) for d in j_to}
    for d in x_to:
        g1[d].wait_recv()

    def mid_b(i, _):
        b.b_mid[i, :, 0:CH] = chosen_prefix(i, slice(0, CH))
        total = b.g_recv[0, lax.div(i, jnp.int32(4))].astype(F32)
        for d in (1, 2, 3):
            total = total + b.g_recv[d, lax.div(i, jnp.int32(4))].astype(F32)
        b.b_mid[i, :, CH : CH + 128] = total.astype(BF16)
        return 0

    lax.fori_loop(0, 8, mid_b, 0)
    b2 = {d: send("b2", d, b.b_mid.at[j_at[d]], b.b_recv2.at[d], j_to[d], mp) for d in j_to}

    for dz in d1:
        d1[dz].wait_recv()
    total = b.d_send[z]
    for dz in d1:
        total = total + b.d_recv[dz]
    b.d_part[...] = total
    dy = send("dy", 0, b.d_part, b.d_other, me, over_y)
    dy.wait_recv()
    total = total + b.d_other[...]
    b.d_sum[...] = total
    b.d_all[z] = total
    d2 = {
        dz: send("d2", dz, b.d_sum, b.d_all.at[z], me, z_at[dz] * 2 + hi) for dz in z_at
    }

    for d in j_to:
        a2[d].wait_recv()
    total = b.a_mid[j].astype(F32)
    for d in j_to:
        total = total + b.a_recv2[d].astype(F32)
    b.cs16[...] = total
    for k in range(3):
        for q in range(4):
            at = 4 * k + q
            b.xpad[5 + k : 6 + k, q * 128 : q * 128 + 128] = b.cs16[at : at + 1, :]
    for dz in d1:
        d1[dz].wait_send()
    pending[:] = [c for c in pending if not any(c is d1[dz] for dz in d1)]
    project_in(16)
    tail = b.d_send[0, :, 256:384]
    b.l_send[...] = jnp.zeros((8, 128), F32)
    for t in range(3):
        b.l_send[2 * t : 2 * t + 1, :] = b.d_send[0, t : t + 1, 0:128]
        b.l_send[2 * t + 1 : 2 * t + 2, :] = b.d_send[0, t : t + 1, 128:256]
    b.l_send[6:7, :] = (
        tail[0:1, :] + pltpu.roll(tail, 32, 1)[1:2, :] + pltpu.roll(tail, 64, 1)[2:3, :]
    )
    l1 = {
        rel: send("l1", rel, b.l_send, b.l_recv.at[rel], me, mp_to[rel]) for rel in mp_to
    }

    oy[1].wait_recv()
    block = b.ow.at[across_y * 2 + core]
    oy[3] = send("oy", 3, block, block, partner, mp)
    osib[1] = send("os", 1, block, block, sibling, mp)

    for name in ("dt_proj", "dt_bias", "a_log", "d_skip", "zin"):
        loads[name].wait()
    for dz in d2:
        d2[dz].wait_recv()
    mask_b = jnp.where(iota((NS, 128), 1) == iota((NS, 128), 0), 1.0, 0.0)
    mask_c = jnp.where(iota((NS, 128), 1) == iota((NS, 128), 0) + NS, 1.0, 0.0)

    def steps(n):
        dbc_in = b.d_all[0 : n // 8, :, 0:DTR].reshape(n, DTR).astype(BF16)
        pre = jnp.dot(dbc_in, b.dt_proj[...], preferred_element_type=F32) + b.dt_bias[...]
        b.dt_s[0:n, :] = jnp.maximum(pre, 0.0) + jnp.log1p(jnp.exp(-jnp.abs(pre)))

    def spread(i, _):
        rows = b.d_all[i, :, DTR : DTR + 128]
        for t in range(8):
            one = jnp.broadcast_to(rows[t : t + 1, :], (NS, 128))
            b.b_exp[i * 8 + t] = jnp.broadcast_to(
                jnp.sum(one * mask_b, axis=1, keepdims=True), (NS, 128)
            )
            b.c_exp[i * 8 + t] = jnp.broadcast_to(
                jnp.sum(one * mask_c, axis=1, keepdims=True), (NS, 128)
            )
        return 0

    steps(SUF)
    lax.fori_loop(1, 8, spread, 0)

    for rel in mp_to:
        l1[rel].wait_recv()
    total = b.l_send[...]
    for rel in mp_to:
        total = total + b.l_recv[rel]
    last = jnp.broadcast_to(total[6:7, :], (8, 128))
    for t in range(3):
        b.d_all[0, t : t + 1, 0:128] = total[2 * t : 2 * t + 1, :]
        b.d_all[0, t : t + 1, 128:256] = total[2 * t + 1 : 2 * t + 2, :]
        moved = pltpu.roll(last, 128 - 32 * t, 1) if t else last
        b.d_all[0, t : t + 1, 256:384] = moved[0:1, :]
    steps(16)
    spread(0, 0)

    for n, line in ((2, beside_y), (3, mod(beside_y + 2, 4))):
        oy[n].wait_recv()
        block = b.ow.at[line * 2 + core]
        osib[n] = send("os", n, block, block, sibling, mp)

    row = iota((128, 1), 0)
    wide = iota((128, 128), 1)
    target = ((row // 4) % 4) * 32 + (row // 16) * 4 + row % 4
    b.perm_rows[...] = jnp.where(wide == target, 1.0, 0.0).astype(BF16)
    target = (row % 16) * 8 + row // 16
    b.perm_small[...] = jnp.where(wide == target, 1.0, 0.0).astype(BF16)
    target = ((row % 32) // 2) * 8 + (row // 32) * 2 + row % 2
    b.perm_out[...] = jnp.where(wide == target, 1.0, 0.0).astype(BF16)
    col = iota((1, 32), 1)
    mine = iota((SUF, 1), 0) == mp * 4 + (col // 2) % 4
    col_group = (col // 8) * 2 + col % 2
    chosen = jnp.zeros((128, 32), F32)
    for k in range(2):
        id_row = jnp.sum(jnp.where(mine, ids[k], 0.0), axis=0, keepdims=True)
        rank_row = jnp.sum(jnp.where(mine, ranks[k], 0.0), axis=0, keepdims=True)
        hit = (
            (row % 8 == col_group)
            & ((row // 16).astype(F32) == id_row)
            & (((row // 8) % 2).astype(F32) == rank_row)
        )
        chosen = chosen + jnp.where(hit, 1.0, 0.0)
    b.sel[...] = chosen.astype(BF16)
    loads["resid"].wait()
    loads["norm_gain"].wait()
    b.r4[...] = b.resid[...].astype(F32)
    for q in range(8):
        for part_ in range(4):
            at = q * 4 + part_
            b.g8[q : q + 1, part_ * 128 : part_ * 128 + 128] = b.norm_gain[at : at + 1, :]
    for px in range(4):
        for t in range(4):
            for half in range(2):
                at, q = t * 2 + half, px * 2 + half
                b.r32[px, at : at + 1, :] = b.r4[t : t + 1, q * 512 : q * 512 + 512]
                b.g32[px, at : at + 1, :] = b.g8[q : q + 1, :]

    for d in j_to:
        b2[d].wait_recv()
    total = b.b_mid[j].astype(F32)
    for d in j_to:
        total = total + b.b_recv2[d].astype(F32)
    gates16 = total[:, CH : CH + 128].astype(BF16)
    amat = -jnp.exp(b.a_log[...])

    def widen(v):
        return jnp.concatenate([v, v, v, v], axis=1)

    def scan8(i, state):
        at = pl.ds(pl.multiple_of(i * 8, 8), 8)
        dt8 = b.dt_s[at, :]
        du8 = dt8 * b.u_s[at, :]
        for t in range(8):
            decay = jnp.exp(dt8[t : t + 1, :] * amat)
            state = decay * state + widen(b.b_exp[i * 8 + t]) * du8[t : t + 1, :]
            b.yv_s[pl.ds(i * 8 + t, 1), :] = jnp.sum(
                widen(b.c_exp[i * 8 + t]) * state, axis=0, keepdims=True
            )
        return state

    yx = {}

    def mixed(half, state):
        state = lax.fori_loop(4 * half, 4 * half + 4, scan8, state)
        at = slice(32 * half, 32 * half + 32)
        gated = (b.yv_s[at, :] + b.d_skip[...] * b.u_s[at, :]) * silu(b.zin[0, at, :].astype(F32))
        ymix = gated.astype(BF16)
        b.ymix[half] = ymix
        b.yfull[half, x] = ymix
        for d in x_to:
            yx[half, d] = send(
                "yx", (half, d), b.ymix.at[half], b.yfull.at[half, x], x_to[d], mp
            )
        return state

    def project_out(half):
        for d in x_to:
            yx[half, d].wait_recv()
        left = jnp.dot(
            b.perm_rows[...], b.yfull[half].reshape(128, CH), preferred_element_type=F32
        ).astype(BF16)
        for n in range(4):
            cols = jnp.concatenate([b.ow[2 * n], b.ow[2 * n + 1]], axis=1)
            part = jnp.dot(left, cols, preferred_element_type=F32).astype(BF16)
            b.p_send[8 * half : 8 * half + 8, :, n * 256 : n * 256 + 256] = part.reshape(
                8, 16, 256
            )

    state = mixed(0, total[:, 0:CH])
    state = mixed(1, state)
    load_o.wait()
    for d in osib:
        osib[d].wait_recv()
    project_out(0)
    project_out(1)

    def send_p(name, at, to_z, dst, dz):
        src = b.p_send.at[pl.ds(2 * to_z, 2)]
        return send(name, at, src, dst, me, z_at[dz] * 2 + hi)

    relay = send_p("p", 4, z_at[4], b.p_relay, 7)
    ps = {dz: send_p("p", dz, z_at[dz], b.p_recv.at[dz], dz) for dz in (3, 6, 2, 7, 1)}
    relay.wait_recv()
    at = pl.ds(2 * z_at[5], 2)
    b.p_send[at] = (b.p_send[at].astype(F32) + b.p_relay[...].astype(F32)).astype(BF16)
    ps[5] = send_p("p", 5, z_at[5], b.p_recv.at[5], 5)
    state_out[...] = state
    for dz in (1, 7, 2, 6, 3, 5):
        ps[dz].wait_recv()

    def part_sum(row):
        total = b.p_send[2 * z + row].astype(F32)
        for dz in ps:
            total = total + b.p_recv[dz, row].astype(F32)
        return total

    b.p_part[...] = part_sum(1 - hi).astype(BF16)
    py = send("py", 0, b.p_part, b.p_other, me, over_y)
    total = part_sum(hi)
    py.wait_recv()
    total = total + b.p_other[...].astype(F32)
    b.p_sum[...] = total
    for px in range(4):
        for t in range(4):
            for half in range(2):
                at = t * 2 + half
                b.hx_send[px, at : at + 1, :] = b.p_sum[
                    px * 4 + t : px * 4 + t + 1, half * 512 : half * 512 + 512
                ]
    hx = {d: send("hx", d, b.hx_send.at[x_at[d]], b.hx_recv.at[x], x_to[d], mp) for d in x_to}
    b.hx_recv[x] = b.hx_send[x]
    for d in x_to:
        hx[d].wait_recv()

    hidden = [b.hx_recv[px] + b.r32[px] for px in range(4)]
    square = hidden[0] * hidden[0]
    for px in range(1, 4):
        square = square + hidden[px] * hidden[px]
    square = jnp.sum(square, axis=1, keepdims=True)
    scales = []
    for t in range(4):
        mean = (square[2 * t : 2 * t + 1] + square[2 * t + 1 : 2 * t + 2]) * (1.0 / D)
        scales += [lax.rsqrt(mean + 1e-05)] * 2
    scale = jnp.concatenate([jnp.broadcast_to(v, (1, 512)) for v in scales], axis=0)
    normed = [hidden[px] * scale * b.g32[px] for px in range(4)]
    b.n32[...] = jnp.concatenate(normed, axis=0).astype(BF16)
    b.e_send[...] = (
        jnp.dot(b.sel[...], b.n32[...], preferred_element_type=F32)
        .astype(BF16)
        .reshape(EXPERTS, 16, 512)
    )

    ex = {
        d: send(
            "ex", d, b.e_send.at[pl.ds(2 * x_at[d], 2)], b.e_mid.at[:, x], x_to[d], mp
        )
        for d in x_to
    }
    b.e_mid[0, x] = b.e_send[2 * x]
    b.e_mid[1, x] = b.e_send[2 * x + 1]
    for px in range(4):
        for t in range(4):
            for half in range(2):
                at, q = t * 2 + half, px * 2 + half
                b.h4[t : t + 1, q * 512 : q * 512 + 512] = hidden[px][at : at + 1, :]
    stream_out[...] = b.h4[...].astype(BF16)
    for d in x_to:
        ex[d].wait_recv()

    kind = mod(pair, 2)

    def send_y(slot, to_y, parity):
        return send(
            "ey",
            slot * 2 + odd,
            b.e_mid.at[parity],
            b.e_recv.at[slot, odd],
            req_of(x, mod(to_y, 4), core),
            z * 2 + lax.div(to_y, jnp.int32(4)),
        )

    send_y(0, yy + 1 - 2 * odd, kind)
    send_y(1, 2 * mod(pair + 1, 4), 1 - kind)
    send_y(1, 2 * mod(pair + 3, 4) + 1, 1 - kind)
    send_y(2, 2 * mod(pair + 2, 4), kind)
    send_y(2, 2 * mod(pair + 2, 4) + 1, kind)
    b.e_recv[0, odd] = b.e_mid[kind]

    def got_y(slot, member):
        pltpu.make_async_remote_copy(
            src_ref=b.e_mid.at[0],
            dst_ref=b.e_recv.at[slot, member],
            send_sem=sems["ey"][0].at[slot * 2 + member],
            recv_sem=sems["ey"][1].at[slot * 2 + member],
            device_id=(me, mp),
            device_id_type=MESH,
        ).wait_recv()

    own_side = 3 - 2 * odd
    chunk = (0, own_side, 2)

    def ring(way, s, i):
        if way == 0:
            block, to = mod(z + 9 - s, 8), mod(z + 1, 8)
        else:
            block, to = mod(z + s - 1, 8), mod(z + 7, 8)
        ref = b.xb.at[block, chunk[i], core]
        return send("zr", (way, s, i), ref, ref, me, to * 2 + hi)

    def in_ring(way, s, i):
        return s <= 3 or (s == 4 and i == way)

    def share(row, block, i):
        ref = b.xb.at[block, chunk[i] if i < 3 else 4 - own_side, core]
        return send("zs", (row, i), ref, ref, sibling, mp)

    def to_pair(row, block):
        ref = b.xb.at[block, own_side, core]
        return send("pr", row, ref, ref, partner, mp)

    block_of = {0: z, 7: mod(z + 4, 8)}
    for s in (1, 2, 3):
        block_of[2 * s - 1] = mod(z + 8 - s, 8)
        block_of[2 * s] = mod(z + s, 8)

    zr, zs, pr = {}, {}, {}
    for i in range(3):
        if i == 0:
            got_y(0, 1 - odd)
        else:
            got_y(i, 0)
            got_y(i, 1)
        raw = b.e_recv[i].reshape(128, 512)
        rows = jnp.dot(b.perm_small[...], raw, preferred_element_type=F32).astype(BF16)
        for q in range(8):
            b.xb[z, chunk[i], core, :, q * 512 : q * 512 + 512] = rows[q * 16 : q * 16 + 16, :]
        zr[0, 1, i] = ring(0, 1, i)
        zr[1, 1, i] = ring(1, 1, i)
        zs[0, i] = share(0, z, i)
        if i == 1:
            pr[0] = to_pair(0, z)

    def handle(s, i):
        for way in (0, 1):
            if (way, s, i) not in zr:
                continue
            zr[way, s, i].wait_recv()
            if in_ring(way, s + 1, i):
                zr[way, s + 1, i] = ring(way, s + 1, i)
            row = 2 * s - 1 + way if s < 4 else 7
            zs[row, i] = share(row, block_of[row], i)
            if i == 1:
                pr[row] = to_pair(row, block_of[row])

    def from_pair(rows):
        for row in rows:
            pr[row].wait_recv()
            zs[row, 3] = share(row, block_of[row], 3)

    i_row = iota((128, 1), 0)
    grp, cc, yi, xs, kk = (
        i_row // 32,
        (i_row // 16) % 2,
        (i_row // 8) % 2,
        (i_row // 2) % 4,
        i_row % 2,
    )
    source = (2 * pair + 2 * grp + yi) % 8
    pick = jnp.where(iota((128, 16), 1) == xs * 4 + source % 4, 1.0, 0.0).astype(BF16)
    spread_g = jnp.dot(pick, gates16, preferred_element_type=F32)
    gate_lane = cc * 64 + (source // 4) * 2 + kk

    def expert(rows):
        for row in rows:
            for i in range(4):
                zs[row, i].wait_recv()
        blocks = [block_of[row] for row in rows]
        m = 128 * len(blocks)
        b.acc_g[0:m, :] = jnp.zeros((m, HID), F32)
        b.acc_u[0:m, :] = jnp.zeros((m, HID), F32)

        def tile(k, _):
            ks = pl.ds(pl.multiple_of(k * KT, KT), KT)
            slots = jnp.concatenate(
                [b.xb[block, :, :, :, ks].reshape(128, KT) for block in blocks], axis=0
            )
            b.acc_g[0:m, :] += jnp.dot(slots, b.w_gate[0, ks, :], preferred_element_type=F32)
            b.acc_u[0:m, :] += jnp.dot(slots, b.w_up[0, ks, :], preferred_element_type=F32)
            return 0

        lax.fori_loop(0, D // KT, tile, 0)
        for n, block in enumerate(blocks):
            here = iota((128, 128), 1) == gate_lane + block * 4
            weight = jnp.sum(jnp.where(here, spread_g, 0.0), axis=1, keepdims=True)
            part = slice(n * 128, n * 128 + 128)
            act = silu(b.acc_g[part, :]) * b.acc_u[part, :] * weight
            for g in range(4):
                for c in range(2):
                    for member in range(2):
                        at = g * 32 + c * 16 + member * 8
                        b.act_s[block, mod(2 * pair + 2 * g + member, 8), c] = act[at : at + 8, :]

    loads["w_gate"].wait()
    loads["w_up"].wait()
    for s in (1, 2, 3):
        for i in range(3):
            handle(s, i)
        if s == 3:
            ref = b.xb.at[mod(z + 5 + core * 6, 8), 2, core]
            z4 = send("z4", 0, ref, ref, me, mod(z + 1 + core * 6, 8) * 2 + hi)
        from_pair([0] if s == 1 else [2 * s - 3, 2 * s - 2])
        if s == 2:
            expert([0])
        if s == 3:
            expert([1, 2])
    handle(4, 0)
    handle(4, 1)
    from_pair([5, 6])
    expert([3, 4])
    z4.wait_recv()
    zs[7, 2] = share(7, block_of[7], 2)
    expert([5, 6])
    from_pair([7])
    expert([7])

    for line in range(4):
        for c in range(2):
            rows = jnp.concatenate(
                [b.act_s[pz, ph * 4 + line, c] for pz in range(8) for ph in range(2)], axis=0
            ).astype(BF16)
            rows = jnp.dot(b.perm_out[...], rows, preferred_element_type=F32).astype(BF16)
            for px in range(4):
                at = ((px * 4 + line) * 2 + c) * 32
                act_out[at : at + 32, :] = rows[px * 32 : px * 32 + 32, :]

    for copy in pending:
        copy.wait_send()


def finish(*refs):
    ins, outs, held, sems = refs[0:3], refs[3:6], refs[6:9], refs[9]
    taken = [pltpu.make_async_copy(ins[n], held[n], sems.at[n]) for n in range(3)]
    given = [pltpu.make_async_copy(held[n], outs[n], sems.at[3 + n]) for n in range(3)]
    for copy in taken:
        copy.start()
    for n in range(3):
        taken[n].wait()
        given[n].start()
    for copy in given:
        copy.wait()


def local(
    xin,
    zin,
    conv_w,
    conv_bias,
    x_proj,
    dt_proj,
    dt_bias,
    a_log,
    d_skip,
    conv_cache,
    ssm_cache,
    prefix_of,
    out_w,
    resid,
    norm_gain,
    expert_ids,
    gate_w,
    w_gate,
    w_up,
):
    operands = {
        "prefix_of": prefix_of,
        "conv_cache": conv_cache.transpose(1, 0, 2),
        "ids": expert_ids.T,
        "gate_w": gate_w.T,
        "ssm_cache": ssm_cache,
        "xin": xin,
        "conv_w": conv_w,
        "conv_bias": conv_bias.reshape(1, CH),
        "x_proj": x_proj.T,
        "resid": resid,
        "norm_gain": norm_gain.reshape(32, 128),
        "dt_proj": dt_proj,
        "dt_bias": dt_bias.reshape(1, CH),
        "a_log": a_log,
        "d_skip": d_skip.reshape(1, CH),
        "zin": zin,
        "w_gate": w_gate,
        "w_up": w_up,
        "out_w": out_w,
    }
    vmem = pl.BlockSpec(memory_space=VMEM)
    dma = pltpu.SemaphoreType.DMA
    sems = []
    for shape in COPIES.values():
        sems += [dma(shape), dma(shape)]
    sems.append(dma((len(LOADED) + 1,)))
    results = (
        jax.ShapeDtypeStruct((4, D), BF16),
        jax.ShapeDtypeStruct((NS, CH), F32),
        jax.ShapeDtypeStruct((1024, HID), BF16),
    )
    made = pl.pallas_call(
        kernel,
        out_shape=results,
        in_specs=[pl.BlockSpec(memory_space=pltpu.HBM)] * len(OPERANDS),
        out_specs=(vmem, vmem, vmem),
        scratch_shapes=list(LOADED.values()) + list(SCRATCH.values()) + sems,
        compiler_params=pltpu.CompilerParams(
            collective_id=0, has_side_effects=True, vmem_limit_bytes=60 * 1024 * 1024
        ),
        name="mixer_and_experts",
    )(*[operands[name] for name in OPERANDS])
    in_hbm = [pl.BlockSpec(memory_space=pltpu.HBM)] * 3
    stream, state, act = pl.pallas_call(
        finish,
        out_shape=results,
        in_specs=in_hbm,
        out_specs=in_hbm,
        scratch_shapes=[VMEM(r.shape, r.dtype) for r in results] + [dma((6,))],
        compiler_params=pltpu.CompilerParams(vmem_limit_bytes=60 * 1024 * 1024),
        name="results",
    )(*made)
    return (stream, state[None], act[None])


def solution(mesh):
    placed = (
        P("req", None, "mp"),
        P("req", None, "mp"),
        P(None, "mp"),
        P("mp"),
        P("mp", None),
        P(None, "mp"),
        P("mp"),
        P(None, "mp"),
        P("mp"),
        P("req", None, "mp"),
        P("req", None, "mp"),
        P(),
        P("mp", "req"),
        P(("req", "mp"), None),
        P(),
        P("req", None),
        P("req", None),
        P("req", None, "mp"),
        P("req", None, "mp"),
    )
    return jax.shard_map(
        local,
        mesh=mesh,
        in_specs=placed,
        out_specs=(P(("req", "mp"), None), P("req", None, "mp"), P("req", None, "mp")),
        check_vma=False,
    )
```

```python
import types

import jax
import jax.numpy as jnp
from jax import lax
from jax.experimental import pallas as pl
from jax.experimental.pallas import tpu as pltpu
from jax.sharding import PartitionSpec as P

F32 = jnp.float32
BF16 = jnp.bfloat16
MESH = pl.DeviceIdType.MESH

D = 4096
CH = 512
NS = 16
SUF = 64
DTR = 256
EXPERTS = 8
HID = 256
KT = 1024

VMEM = pltpu.VMEM
LOADED = {
    "prefix_of": pltpu.SMEM((32,), jnp.int32),
    "conv_cache": VMEM((3, 2, CH), F32),
    "ids": VMEM((2, SUF), jnp.int32),
    "gate_w": VMEM((2, SUF), BF16),
    "ssm_cache": VMEM((2, NS, CH), F32),
    "xin": VMEM((1, SUF, CH), BF16),
    "conv_w": VMEM((4, CH), F32),
    "conv_bias": VMEM((1, CH), F32),
    "x_proj": VMEM((DTR + 2 * NS, CH), BF16),
    "resid": VMEM((4, D), BF16),
    "norm_gain": VMEM((32, 128), F32),
    "dt_proj": VMEM((DTR, CH), BF16),
    "dt_bias": VMEM((1, CH), F32),
    "a_log": VMEM((NS, CH), F32),
    "d_skip": VMEM((1, CH), F32),
    "zin": VMEM((1, SUF, CH), BF16),
    "w_gate": VMEM((1, D, HID), BF16),
    "w_up": VMEM((1, D, HID), BF16),
}
SCRATCH = {
    "cc16": VMEM((2, 16, 128), F32),
    "cs16": VMEM((16, 128), F32),
    "xpad": VMEM((72, CH), F32),
    "c_send": VMEM((2, 16, CH + 128), BF16),
    "c_recv": VMEM((4, 2, 16, CH + 128), BF16),
    "g_recv": VMEM((4, 2, 16, 128), BF16),
    "a_mid": VMEM((8, 16, 128), BF16),
    "a_recv2": VMEM((8, 16, 128), BF16),
    "b_mid": VMEM((8, 16, CH + 128), BF16),
    "b_recv2": VMEM((8, 16, CH + 128), BF16),
    "gmat": VMEM((8, 16, 128), BF16),
    "d_send": VMEM((8, 8, 384), F32),
    "d_recv": VMEM((8, 8, 384), F32),
    "d_part": VMEM((8, 384), F32),
    "d_other": VMEM((8, 384), F32),
    "d_sum": VMEM((8, 384), F32),
    "d_all": VMEM((8, 8, 384), F32),
    "l_send": VMEM((8, 128), F32),
    "l_recv": VMEM((16, 8, 128), F32),
    "dt_s": VMEM((SUF, CH), F32),
    "u_s": VMEM((SUF, CH), F32),
    "yv_s": VMEM((SUF, CH), F32),
    "b_exp": VMEM((SUF, NS, 128), F32),
    "c_exp": VMEM((SUF, NS, 128), F32),
    "ow": VMEM((8, CH, 128), BF16),
    "ymix": VMEM((2, 32, CH), BF16),
    "yfull": VMEM((2, 4, 32, CH), BF16),
    "perm_rows": VMEM((128, 128), BF16),
    "perm_out": VMEM((128, 128), BF16),
    "perm_small": VMEM((128, 128), BF16),
    "p_send": VMEM((16, 16, 1024), BF16),
    "p_recv": VMEM((8, 2, 16, 1024), BF16),
    "p_relay": VMEM((2, 16, 1024), BF16),
    "p_part": VMEM((16, 1024), BF16),
    "p_other": VMEM((16, 1024), BF16),
    "p_sum": VMEM((16, 1024), F32),
    "hx_send": VMEM((4, 8, 512), F32),
    "hx_recv": VMEM((4, 8, 512), F32),
    "r4": VMEM((4, D), F32),
    "r32": VMEM((4, 8, 512), F32),
    "g8": VMEM((8, 512), F32),
    "g32": VMEM((4, 8, 512), F32),
    "n32": VMEM((32, 512), BF16),
    "h4": VMEM((4, D), F32),
    "sel": VMEM((128, 32), BF16),
    "e_send": VMEM((8, 16, 512), BF16),
    "e_mid": VMEM((2, 4, 16, 512), BF16),
    "e_recv": VMEM((3, 2, 4, 16, 512), BF16),
    "xb": VMEM((8, 4, 2, 16, D), BF16),
    "acc_g": VMEM((256, HID), F32),
    "acc_u": VMEM((256, HID), F32),
    "act_s": VMEM((8, 8, 2, 8, HID), F32),
}
COPIES = {
    "c1": (4,),
    "g1": (4,),
    "a2": (8,),
    "b2": (8,),
    "d1": (8,),
    "dy": (1,),
    "d2": (8,),
    "l1": (16,),
    "oy": (4,),
    "os": (4,),
    "yx": (2, 4),
    "p": (8,),
    "py": (1,),
    "hx": (4,),
    "ex": (4,),
    "ey": (6,),
    "zr": (2, 5, 3),
    "z4": (1,),
    "pr": (8,),
    "zs": (8, 4),
}
OPERANDS = list(LOADED) + ["out_w"]
BUFFERS = list(LOADED) + list(SCRATCH)


def mod(a, n):
    return lax.rem(a, jnp.int32(n))


def iota(shape, dim):
    return lax.broadcasted_iota(jnp.int32, shape, dim)


def silu(v):
    return v / (1.0 + jnp.exp(-v))


def kernel(*refs):
    hbm = dict(zip(OPERANDS, refs))
    refs = refs[len(OPERANDS) :]
    stream_out, state_out, act_out = refs[:3]
    refs = refs[3:]
    b = types.SimpleNamespace(**dict(zip(BUFFERS, refs)))
    refs = refs[len(BUFFERS) :]
    sems = {name: (refs[2 * n], refs[2 * n + 1]) for n, name in enumerate(COPIES)}
    loc = refs[2 * len(COPIES)]

    me = lax.axis_index("req")
    mp = lax.axis_index("mp")
    x = lax.div(me, jnp.int32(8))
    j = mod(me, 8)
    ylo = lax.div(j, jnp.int32(2))
    core = mod(me, 2)
    z = lax.div(mp, jnp.int32(2))
    hi = mod(mp, 2)
    yy = hi * 4 + ylo
    odd = mod(ylo, 2)
    pair = lax.div(yy, jnp.int32(2))
    z_at = {dz: mod(z + dz, 8) for dz in range(1, 8)}
    over_y = z * 2 + 1 - hi

    def req_of(px, pylo, pcore):
        return px * 8 + pylo * 2 + pcore

    pending = []

    def send(name, at, src, dst, to_req, to_mp):
        copy = pltpu.make_async_remote_copy(
            src_ref=src,
            dst_ref=dst,
            send_sem=sems[name][0].at[at],
            recv_sem=sems[name][1].at[at],
            device_id=(to_req, to_mp),
            device_id_type=MESH,
        )
        copy.start()
        pending.append(copy)
        return copy

    loads = {}
    for n, name in enumerate(LOADED):
        loads[name] = pltpu.make_async_copy(hbm[name], getattr(b, name), loc.at[n])
        loads[name].start()
    load_o = pltpu.make_async_copy(hbm["out_w"], b.ow.at[j], loc.at[len(LOADED)])
    load_o.start()

    x_at = {d: mod(x + d, 4) for d in (1, 2, 3)}
    j_at = {d: mod(j + d, 8) for d in range(1, 8)}
    x_to = {d: req_of(x_at[d], ylo, core) for d in (1, 2, 3)}
    j_to = {d: x * 8 + j_at[d] for d in range(1, 8)}
    mp_to = {}
    for dz in range(8):
        for dh in range(2):
            if dz or dh:
                mp_to[dz * 2 + dh] = mod(z + dz, 8) * 2 + mod(hi + dh, 2)
    sibling = req_of(x, ylo, 1 - core)
    partner = req_of(x, ylo + 1 - 2 * odd, core)

    barrier = pltpu.get_barrier_semaphore()
    greet = [(x_to[d], mp) for d in x_to]
    greet += [(j_to[d], mp) for d in j_to]
    greet += [(me, mp_to[d]) for d in mp_to]
    greet += [(req_of(x, mod(ylo + d, 4), core), z * 2 + 1 - hi) for d in (1, 2, 3)]
    for to in greet:
        pl.semaphore_signal(barrier, inc=1, device_id=to, device_id_type=MESH)

    b.cc16[...] = jnp.zeros_like(b.cc16)
    loads["prefix_of"].wait()
    loads["conv_cache"].wait()
    for s in range(2):
        for k in range(3):
            for q in range(4):
                at = 4 * k + q
                b.cc16[s, at : at + 1, :] = b.conv_cache[k, s : s + 1, q * 128 : q * 128 + 128]

    loads["ssm_cache"].wait()
    for s in range(2):
        b.c_send[s, :, 0:CH] = b.ssm_cache[s].astype(BF16)
        b.c_send[s, :, CH : CH + 128] = b.cc16[s].astype(BF16)
    b.c_recv[0] = b.c_send[...]

    loads["xin"].wait()
    b.xpad[0:8, :] = jnp.zeros((8, CH), F32)
    b.xpad[8 : 8 + SUF, :] = b.xin[0].astype(F32)
    b.d_send[:, :, 256:384] = jnp.zeros((8, 8, 128), F32)
    for name in ("conv_w", "conv_bias", "x_proj"):
        loads[name].wait()
    rows_by_rows = (((1,), (1,)), ((), ()))

    def project_in(n):
        conv = b.conv_w[0:1, :] * b.xpad[5 : 5 + n, :]
        for k in range(1, 4):
            conv = conv + b.conv_w[k : k + 1, :] * b.xpad[5 + k : 5 + k + n, :]
        u16 = silu(conv + b.conv_bias[...]).astype(BF16)
        b.u_s[0:n, :] = u16.astype(F32)
        part = lax.dot_general(u16, b.x_proj[0:DTR, :], rows_by_rows, preferred_element_type=F32)
        part_bc = lax.dot_general(
            u16, b.x_proj[DTR : DTR + 2 * NS, :], rows_by_rows, preferred_element_type=F32
        )
        b.d_send[0 : n // 8, :, 0:DTR] = part.reshape(n // 8, 8, DTR)
        b.d_send[0 : n // 8, :, DTR : DTR + 2 * NS] = part_bc.reshape(n // 8, 8, 2 * NS)

    project_in(SUF)
    pl.semaphore_wait(barrier, len(greet))
    c1 = {d: send("c1", d, b.c_send, b.c_recv.at[d], x_to[d], mp) for d in x_to}
    d1 = {
        dz: send("d1", dz, b.d_send.at[z_at[dz]], b.d_recv.at[dz], me, z_at[dz] * 2 + hi)
        for dz in z_at
    }
    across_y = mod(ylo + 2, 4)
    beside_y = ylo + 1 - 2 * odd
    oy = {
        1: send("oy", 1, hbm["out_w"], b.ow.at[j], req_of(x, across_y, core), mp),
        2: send("oy", 2, hbm["out_w"], b.ow.at[j], partner, mp),
    }
    osib = {0: send("os", 0, hbm["out_w"], b.ow.at[j], sibling, mp)}

    loads["ids"].wait()
    loads["gate_w"].wait()
    eye = iota((SUF, SUF), 0) == iota((SUF, SUF), 1)

    def column(row):
        return jnp.sum(jnp.where(eye, row, 0.0), axis=1, keepdims=True)

    id_rows = b.ids[...].astype(F32)
    gate_rows = b.gate_w[...].astype(F32)
    ids = [column(id_rows[k : k + 1, :]) for k in range(2)]
    gates = [column(gate_rows[k : k + 1, :]) for k in range(2)]
    lane8 = iota((SUF, 128), 1).astype(F32)
    onehot = (
        jnp.where(ids[0] == lane8, 1.0, 0.0) + jnp.where(ids[1] == lane8, 1.0, 0.0)
    ).astype(BF16)
    tri_r, tri_c = iota((SUF, 1), 0), iota((1, SUF), 1)
    tri = jnp.where((tri_r // 4 == tri_c // 4) & (tri_c < tri_r), 1.0, 0.0).astype(BF16)
    before = jnp.dot(tri, onehot, preferred_element_type=F32)
    ranks = [
        jnp.sum(jnp.where(ids[k] == lane8, before, 0.0), axis=1, keepdims=True) for k in range(2)
    ]
    lane = iota((1, 128), 1)
    lane_block = jnp.where((lane % 64 < 32) & (lane // 64 == core), (lane % 64) // 2, -1)
    place = iota((SUF, 1), 0) // 4 == lane_block
    lane_rank = (lane % 2).astype(F32)
    row16 = iota((16, 128), 0)

    def fill_g(e, _):
        total = jnp.zeros((1, 128), F32)
        for k in range(2):
            hit = place & (ids[k] == e.astype(F32)) & (ranks[k] == lane_rank)
            total = total + jnp.sum(jnp.where(hit, gates[k], 0.0), axis=0, keepdims=True)
        b.gmat[e] = jnp.where(
            row16 == lax.div(me, jnp.int32(2)), jnp.broadcast_to(total, (16, 128)), 0.0
        ).astype(BF16)
        return 0

    lax.fori_loop(0, EXPERTS, fill_g, 0)

    b.g_recv[0, 0] = b.gmat[2 * x]
    b.g_recv[0, 1] = b.gmat[2 * x + 1]

    g1 = {
        d: send("g1", d, b.gmat.at[pl.ds(2 * x_at[d], 2)], b.g_recv.at[d], x_to[d], mp)
        for d in x_to
    }

    for d in x_to:
        c1[d].wait_recv()

    def chosen_prefix(i, lanes):
        p = b.prefix_of[x * 8 + i]
        total = jnp.zeros((16, lanes.stop - lanes.start), F32)
        for d in range(4):
            owner = mod(x + 4 - d, 4) * 8 + j
            for s in range(2):
                here = jnp.where(p == 2 * owner + s, 1.0, 0.0).astype(F32)
                total = total + b.c_recv[d, s, :, lanes].astype(F32) * here
        return total.astype(BF16)

    def mid_a(i, _):
        b.a_mid[i] = chosen_prefix(i, slice(CH, CH + 128))
        return 0

    lax.fori_loop(0, 8, mid_a, 0)
    a2 = {d: send("a2", d, b.a_mid.at[j_at[d]], b.a_recv2.at[d], j_to[d], mp) for d in j_to}
    for d in x_to:
        g1[d].wait_recv()

    def mid_b(i, _):
        b.b_mid[i, :, 0:CH] = chosen_prefix(i, slice(0, CH))
        total = b.g_recv[0, lax.div(i, jnp.int32(4))].astype(F32)
        for d in (1, 2, 3):
            total = total + b.g_recv[d, lax.div(i, jnp.int32(4))].astype(F32)
        b.b_mid[i, :, CH : CH + 128] = total.astype(BF16)
        return 0

    lax.fori_loop(0, 8, mid_b, 0)
    b2 = {d: send("b2", d, b.b_mid.at[j_at[d]], b.b_recv2.at[d], j_to[d], mp) for d in j_to}

    for dz in d1:
        d1[dz].wait_recv()
    total = b.d_send[z]
    for dz in d1:
        total = total + b.d_recv[dz]
    b.d_part[...] = total
    dy = send("dy", 0, b.d_part, b.d_other, me, over_y)
    dy.wait_recv()
    total = total + b.d_other[...]
    b.d_sum[...] = total
    b.d_all[z] = total
    d2 = {
        dz: send("d2", dz, b.d_sum, b.d_all.at[z], me, z_at[dz] * 2 + hi) for dz in z_at
    }

    for d in j_to:
        a2[d].wait_recv()
    total = b.a_mid[j].astype(F32)
    for d in j_to:
        total = total + b.a_recv2[d].astype(F32)
    b.cs16[...] = total
    for k in range(3):
        for q in range(4):
            at = 4 * k + q
            b.xpad[5 + k : 6 + k, q * 128 : q * 128 + 128] = b.cs16[at : at + 1, :]
    for dz in d1:
        d1[dz].wait_send()
    pending[:] = [c for c in pending if not any(c is d1[dz] for dz in d1)]
    project_in(16)
    tail = b.d_send[0, :, 256:384]
    b.l_send[...] = jnp.zeros((8, 128), F32)
    for t in range(3):
        b.l_send[2 * t : 2 * t + 1, :] = b.d_send[0, t : t + 1, 0:128]
        b.l_send[2 * t + 1 : 2 * t + 2, :] = b.d_send[0, t : t + 1, 128:256]
    b.l_send[6:7, :] = (
        tail[0:1, :] + pltpu.roll(tail, 32, 1)[1:2, :] + pltpu.roll(tail, 64, 1)[2:3, :]
    )
    l1 = {
        rel: send("l1", rel, b.l_send, b.l_recv.at[rel], me, mp_to[rel]) for rel in mp_to
    }

    oy[1].wait_recv()
    block = b.ow.at[across_y * 2 + core]
    oy[3] = send("oy", 3, block, block, partner, mp)
    osib[1] = send("os", 1, block, block, sibling, mp)

    for name in ("dt_proj", "dt_bias", "a_log", "d_skip", "zin"):
        loads[name].wait()
    for dz in d2:
        d2[dz].wait_recv()
    mask_b = jnp.where(iota((NS, 128), 1) == iota((NS, 128), 0), 1.0, 0.0)
    mask_c = jnp.where(iota((NS, 128), 1) == iota((NS, 128), 0) + NS, 1.0, 0.0)

    def steps(n):
        dbc_in = b.d_all[0 : n // 8, :, 0:DTR].reshape(n, DTR).astype(BF16)
        pre = jnp.dot(dbc_in, b.dt_proj[...], preferred_element_type=F32) + b.dt_bias[...]
        b.dt_s[0:n, :] = jnp.maximum(pre, 0.0) + jnp.log1p(jnp.exp(-jnp.abs(pre)))

    def spread(i, _):
        rows = b.d_all[i, :, DTR : DTR + 128]
        for t in range(8):
            one = jnp.broadcast_to(rows[t : t + 1, :], (NS, 128))
            b.b_exp[i * 8 + t] = jnp.broadcast_to(
                jnp.sum(one * mask_b, axis=1, keepdims=True), (NS, 128)
            )
            b.c_exp[i * 8 + t] = jnp.broadcast_to(
                jnp.sum(one * mask_c, axis=1, keepdims=True), (NS, 128)
            )
        return 0

    steps(SUF)
    lax.fori_loop(1, 8, spread, 0)

    for rel in mp_to:
        l1[rel].wait_recv()
    total = b.l_send[...]
    for rel in mp_to:
        total = total + b.l_recv[rel]
    last = jnp.broadcast_to(total[6:7, :], (8, 128))
    for t in range(3):
        b.d_all[0, t : t + 1, 0:128] = total[2 * t : 2 * t + 1, :]
        b.d_all[0, t : t + 1, 128:256] = total[2 * t + 1 : 2 * t + 2, :]
        moved = pltpu.roll(last, 128 - 32 * t, 1) if t else last
        b.d_all[0, t : t + 1, 256:384] = moved[0:1, :]
    steps(16)
    spread(0, 0)

    for n, line in ((2, beside_y), (3, mod(beside_y + 2, 4))):
        oy[n].wait_recv()
        block = b.ow.at[line * 2 + core]
        osib[n] = send("os", n, block, block, sibling, mp)

    row = iota((128, 1), 0)
    wide = iota((128, 128), 1)
    target = ((row // 4) % 4) * 32 + (row // 16) * 4 + row % 4
    b.perm_rows[...] = jnp.where(wide == target, 1.0, 0.0).astype(BF16)
    target = (row % 16) * 8 + row // 16
    b.perm_small[...] = jnp.where(wide == target, 1.0, 0.0).astype(BF16)
    target = ((row % 32) // 2) * 8 + (row // 32) * 2 + row % 2
    b.perm_out[...] = jnp.where(wide == target, 1.0, 0.0).astype(BF16)
    col = iota((1, 32), 1)
    mine = iota((SUF, 1), 0) == mp * 4 + (col // 2) % 4
    col_group = (col // 8) * 2 + col % 2
    chosen = jnp.zeros((128, 32), F32)
    for k in range(2):
        id_row = jnp.sum(jnp.where(mine, ids[k], 0.0), axis=0, keepdims=True)
        rank_row = jnp.sum(jnp.where(mine, ranks[k], 0.0), axis=0, keepdims=True)
        hit = (
            (row % 8 == col_group)
            & ((row // 16).astype(F32) == id_row)
            & (((row // 8) % 2).astype(F32) == rank_row)
        )
        chosen = chosen + jnp.where(hit, 1.0, 0.0)
    b.sel[...] = chosen.astype(BF16)
    loads["resid"].wait()
    loads["norm_gain"].wait()
    b.r4[...] = b.resid[...].astype(F32)
    for q in range(8):
        for part_ in range(4):
            at = q * 4 + part_
            b.g8[q : q + 1, part_ * 128 : part_ * 128 + 128] = b.norm_gain[at : at + 1, :]
    for px in range(4):
        for t in range(4):
            for half in range(2):
                at, q = t * 2 + half, px * 2 + half
                b.r32[px, at : at + 1, :] = b.r4[t : t + 1, q * 512 : q * 512 + 512]
                b.g32[px, at : at + 1, :] = b.g8[q : q + 1, :]

    for d in j_to:
        b2[d].wait_recv()
    total = b.b_mid[j].astype(F32)
    for d in j_to:
        total = total + b.b_recv2[d].astype(F32)
    gates16 = total[:, CH : CH + 128].astype(BF16)
    amat = -jnp.exp(b.a_log[...])

    def widen(v):
        return jnp.concatenate([v, v, v, v], axis=1)

    def scan8(i, state):
        at = pl.ds(pl.multiple_of(i * 8, 8), 8)
        dt8 = b.dt_s[at, :]
        du8 = dt8 * b.u_s[at, :]
        for t in range(8):
            decay = jnp.exp(dt8[t : t + 1, :] * amat)
            state = decay * state + widen(b.b_exp[i * 8 + t]) * du8[t : t + 1, :]
            b.yv_s[pl.ds(i * 8 + t, 1), :] = jnp.sum(
                widen(b.c_exp[i * 8 + t]) * state, axis=0, keepdims=True
            )
        return state

    yx = {}

    def mixed(half, state):
        state = lax.fori_loop(4 * half, 4 * half + 4, scan8, state)
        at = slice(32 * half, 32 * half + 32)
        gated = (b.yv_s[at, :] + b.d_skip[...] * b.u_s[at, :]) * silu(b.zin[0, at, :].astype(F32))
        ymix = gated.astype(BF16)
        b.ymix[half] = ymix
        b.yfull[half, x] = ymix
        for d in x_to:
            yx[half, d] = send(
                "yx", (half, d), b.ymix.at[half], b.yfull.at[half, x], x_to[d], mp
            )
        return state

    def project_out(half):
        for d in x_to:
            yx[half, d].wait_recv()
        left = jnp.dot(
            b.perm_rows[...], b.yfull[half].reshape(128, CH), preferred_element_type=F32
        ).astype(BF16)
        for n in range(4):
            cols = jnp.concatenate([b.ow[2 * n], b.ow[2 * n + 1]], axis=1)
            part = jnp.dot(left, cols, preferred_element_type=F32).astype(BF16)
            b.p_send[8 * half : 8 * half + 8, :, n * 256 : n * 256 + 256] = part.reshape(
                8, 16, 256
            )

    state = mixed(0, total[:, 0:CH])
    state = mixed(1, state)
    load_o.wait()
    for d in osib:
        osib[d].wait_recv()
    project_out(0)
    project_out(1)

    def send_p(name, at, to_z, dst, dz):
        src = b.p_send.at[pl.ds(2 * to_z, 2)]
        return send(name, at, src, dst, me, z_at[dz] * 2 + hi)

    relay = send_p("p", 4, z_at[4], b.p_relay, 7)
    ps = {dz: send_p("p", dz, z_at[dz], b.p_recv.at[dz], dz) for dz in (3, 6, 2, 7, 1)}
    relay.wait_recv()
    at = pl.ds(2 * z_at[5], 2)
    b.p_send[at] = (b.p_send[at].astype(F32) + b.p_relay[...].astype(F32)).astype(BF16)
    ps[5] = send_p("p", 5, z_at[5], b.p_recv.at[5], 5)
    state_out[...] = state
    for dz in (1, 7, 2, 6, 3, 5):
        ps[dz].wait_recv()

    def part_sum(row):
        total = b.p_send[2 * z + row].astype(F32)
        for dz in ps:
            total = total + b.p_recv[dz, row].astype(F32)
        return total

    b.p_part[...] = part_sum(1 - hi).astype(BF16)
    py = send("py", 0, b.p_part, b.p_other, me, over_y)
    total = part_sum(hi)
    py.wait_recv()
    total = total + b.p_other[...].astype(F32)
    b.p_sum[...] = total
    for px in range(4):
        for t in range(4):
            for half in range(2):
                at = t * 2 + half
                b.hx_send[px, at : at + 1, :] = b.p_sum[
                    px * 4 + t : px * 4 + t + 1, half * 512 : half * 512 + 512
                ]
    hx = {d: send("hx", d, b.hx_send.at[x_at[d]], b.hx_recv.at[x], x_to[d], mp) for d in x_to}
    b.hx_recv[x] = b.hx_send[x]
    for d in x_to:
        hx[d].wait_recv()

    hidden = [b.hx_recv[px] + b.r32[px] for px in range(4)]
    square = hidden[0] * hidden[0]
    for px in range(1, 4):
        square = square + hidden[px] * hidden[px]
    square = jnp.sum(square, axis=1, keepdims=True)
    scales = []
    for t in range(4):
        mean = (square[2 * t : 2 * t + 1] + square[2 * t + 1 : 2 * t + 2]) * (1.0 / D)
        scales += [lax.rsqrt(mean + 1e-05)] * 2
    scale = jnp.concatenate([jnp.broadcast_to(v, (1, 512)) for v in scales], axis=0)
    normed = [hidden[px] * scale * b.g32[px] for px in range(4)]
    b.n32[...] = jnp.concatenate(normed, axis=0).astype(BF16)
    b.e_send[...] = (
        jnp.dot(b.sel[...], b.n32[...], preferred_element_type=F32)
        .astype(BF16)
        .reshape(EXPERTS, 16, 512)
    )

    ex = {
        d: send(
            "ex", d, b.e_send.at[pl.ds(2 * x_at[d], 2)], b.e_mid.at[:, x], x_to[d], mp
        )
        for d in x_to
    }
    b.e_mid[0, x] = b.e_send[2 * x]
    b.e_mid[1, x] = b.e_send[2 * x + 1]
    for px in range(4):
        for t in range(4):
            for half in range(2):
                at, q = t * 2 + half, px * 2 + half
                b.h4[t : t + 1, q * 512 : q * 512 + 512] = hidden[px][at : at + 1, :]
    stream_out[...] = b.h4[...].astype(BF16)
    for d in x_to:
        ex[d].wait_recv()

    kind = mod(pair, 2)

    def send_y(slot, to_y, parity):
        return send(
            "ey",
            slot * 2 + odd,
            b.e_mid.at[parity],
            b.e_recv.at[slot, odd],
            req_of(x, mod(to_y, 4), core),
            z * 2 + lax.div(to_y, jnp.int32(4)),
        )

    send_y(0, yy + 1 - 2 * odd, kind)
    send_y(1, 2 * mod(pair + 1, 4), 1 - kind)
    send_y(1, 2 * mod(pair + 3, 4) + 1, 1 - kind)
    send_y(2, 2 * mod(pair + 2, 4) + 1 - odd, kind)
    b.e_recv[0, odd] = b.e_mid[kind]

    def got_y(slot, member):
        pltpu.make_async_remote_copy(
            src_ref=b.e_mid.at[0],
            dst_ref=b.e_recv.at[slot, member],
            send_sem=sems["ey"][0].at[slot * 2 + member],
            recv_sem=sems["ey"][1].at[slot * 2 + member],
            device_id=(me, mp),
            device_id_type=MESH,
        ).wait_recv()

    own_side = 3 - 2 * odd
    chunk = (0, own_side, 2)

    def ring(way, s, i):
        if way == 0:
            block, to = mod(z + 9 - s, 8), mod(z + 1, 8)
        else:
            block, to = mod(z + s - 1, 8), mod(z + 7, 8)
        ref = b.xb.at[block, chunk[i], core]
        return send("zr", (way, s, i), ref, ref, me, to * 2 + hi)

    def in_ring(way, s, i):
        return s <= 3 or (s == 4 and i == way)

    def share(row, block, i):
        ref = b.xb.at[block, chunk[i] if i < 3 else 4 - own_side, core]
        return send("zs", (row, i), ref, ref, sibling, mp)

    def to_pair(row, block):
        ref = b.xb.at[block, own_side, core]
        return send("pr", row, ref, ref, partner, mp)

    block_of = {0: z, 7: mod(z + 4, 8)}
    for s in (1, 2, 3):
        block_of[2 * s - 1] = mod(z + 8 - s, 8)
        block_of[2 * s] = mod(z + s, 8)

    zr, zs, pr = {}, {}, {}
    for i in range(3):
        if i == 0:
            got_y(0, 1 - odd)
        elif i == 1:
            got_y(1, 0)
            got_y(1, 1)
        else:
            got_y(2, 1 - odd)
            block = b.e_recv.at[2, 1 - odd]
            send("ey", 5 - odd, block, block, partner, mp)
            got_y(2, odd)
        raw = b.e_recv[i].reshape(128, 512)
        rows = jnp.dot(b.perm_small[...], raw, preferred_element_type=F32).astype(BF16)
        for q in range(8):
            b.xb[z, chunk[i], core, :, q * 512 : q * 512 + 512] = rows[q * 16 : q * 16 + 16, :]
        zr[0, 1, i] = ring(0, 1, i)
        zr[1, 1, i] = ring(1, 1, i)
        zs[0, i] = share(0, z, i)
        if i == 1:
            pr[0] = to_pair(0, z)

    def handle(s, i):
        for way in (0, 1):
            if (way, s, i) not in zr:
                continue
            zr[way, s, i].wait_recv()
            if in_ring(way, s + 1, i):
                zr[way, s + 1, i] = ring(way, s + 1, i)
            row = 2 * s - 1 + way if s < 4 else 7
            zs[row, i] = share(row, block_of[row], i)
            if i == 1:
                pr[row] = to_pair(row, block_of[row])

    def from_pair(rows):
        for row in rows:
            pr[row].wait_recv()
            zs[row, 3] = share(row, block_of[row], 3)

    i_row = iota((128, 1), 0)
    grp, cc, yi, xs, kk = (
        i_row // 32,
        (i_row // 16) % 2,
        (i_row // 8) % 2,
        (i_row // 2) % 4,
        i_row % 2,
    )
    source = (2 * pair + 2 * grp + yi) % 8
    pick = jnp.where(iota((128, 16), 1) == xs * 4 + source % 4, 1.0, 0.0).astype(BF16)
    spread_g = jnp.dot(pick, gates16, preferred_element_type=F32)
    gate_lane = cc * 64 + (source // 4) * 2 + kk

    def expert(rows):
        for row in rows:
            for i in range(4):
                zs[row, i].wait_recv()
        blocks = [block_of[row] for row in rows]
        m = 128 * len(blocks)
        b.acc_g[0:m, :] = jnp.zeros((m, HID), F32)
        b.acc_u[0:m, :] = jnp.zeros((m, HID), F32)

        def tile(k, _):
            ks = pl.ds(pl.multiple_of(k * KT, KT), KT)
            slots = jnp.concatenate(
                [b.xb[block, :, :, :, ks].reshape(128, KT) for block in blocks], axis=0
            )
            b.acc_g[0:m, :] += jnp.dot(slots, b.w_gate[0, ks, :], preferred_element_type=F32)
            b.acc_u[0:m, :] += jnp.dot(slots, b.w_up[0, ks, :], preferred_element_type=F32)
            return 0

        lax.fori_loop(0, D // KT, tile, 0)
        for n, block in enumerate(blocks):
            here = iota((128, 128), 1) == gate_lane + block * 4
            weight = jnp.sum(jnp.where(here, spread_g, 0.0), axis=1, keepdims=True)
            part = slice(n * 128, n * 128 + 128)
            act = silu(b.acc_g[part, :]) * b.acc_u[part, :] * weight
            for g in range(4):
                for c in range(2):
                    for member in range(2):
                        at = g * 32 + c * 16 + member * 8
                        b.act_s[block, mod(2 * pair + 2 * g + member, 8), c] = act[at : at + 8, :]

    loads["w_gate"].wait()
    loads["w_up"].wait()
    for s in (1, 2, 3):
        for i in range(3):
            handle(s, i)
        if s == 3:
            ref = b.xb.at[mod(z + 5 + core * 6, 8), 2, core]
            z4 = send("z4", 0, ref, ref, me, mod(z + 1 + core * 6, 8) * 2 + hi)
        from_pair([0] if s == 1 else [2 * s - 3, 2 * s - 2])
        if s == 2:
            expert([0])
        if s == 3:
            expert([1, 2])
    handle(4, 0)
    handle(4, 1)
    from_pair([5, 6])
    expert([3, 4])
    z4.wait_recv()
    zs[7, 2] = share(7, block_of[7], 2)
    expert([5, 6])
    from_pair([7])
    expert([7])

    for line in range(4):
        for c in range(2):
            rows = jnp.concatenate(
                [b.act_s[pz, ph * 4 + line, c] for pz in range(8) for ph in range(2)], axis=0
            ).astype(BF16)
            rows = jnp.dot(b.perm_out[...], rows, preferred_element_type=F32).astype(BF16)
            for px in range(4):
                at = ((px * 4 + line) * 2 + c) * 32
                act_out[at : at + 32, :] = rows[px * 32 : px * 32 + 32, :]

    for copy in pending:
        copy.wait_send()


def finish(*refs):
    ins, outs, held, sems = refs[0:3], refs[3:6], refs[6:9], refs[9]
    taken = [pltpu.make_async_copy(ins[n], held[n], sems.at[n]) for n in range(3)]
    given = [pltpu.make_async_copy(held[n], outs[n], sems.at[3 + n]) for n in range(3)]
    for copy in taken:
        copy.start()
    for n in range(3):
        taken[n].wait()
        given[n].start()
    for copy in given:
        copy.wait()


def local(
    xin,
    zin,
    conv_w,
    conv_bias,
    x_proj,
    dt_proj,
    dt_bias,
    a_log,
    d_skip,
    conv_cache,
    ssm_cache,
    prefix_of,
    out_w,
    resid,
    norm_gain,
    expert_ids,
    gate_w,
    w_gate,
    w_up,
):
    operands = {
        "prefix_of": prefix_of,
        "conv_cache": conv_cache.transpose(1, 0, 2),
        "ids": expert_ids.T,
        "gate_w": gate_w.T,
        "ssm_cache": ssm_cache,
        "xin": xin,
        "conv_w": conv_w,
        "conv_bias": conv_bias.reshape(1, CH),
        "x_proj": x_proj.T,
        "resid": resid,
        "norm_gain": norm_gain.reshape(32, 128),
        "dt_proj": dt_proj,
        "dt_bias": dt_bias.reshape(1, CH),
        "a_log": a_log,
        "d_skip": d_skip.reshape(1, CH),
        "zin": zin,
        "w_gate": w_gate,
        "w_up": w_up,
        "out_w": out_w,
    }
    vmem = pl.BlockSpec(memory_space=VMEM)
    dma = pltpu.SemaphoreType.DMA
    sems = []
    for shape in COPIES.values():
        sems += [dma(shape), dma(shape)]
    sems.append(dma((len(LOADED) + 1,)))
    results = (
        jax.ShapeDtypeStruct((4, D), BF16),
        jax.ShapeDtypeStruct((NS, CH), F32),
        jax.ShapeDtypeStruct((1024, HID), BF16),
    )
    made = pl.pallas_call(
        kernel,
        out_shape=results,
        in_specs=[pl.BlockSpec(memory_space=pltpu.HBM)] * len(OPERANDS),
        out_specs=(vmem, vmem, vmem),
        scratch_shapes=list(LOADED.values()) + list(SCRATCH.values()) + sems,
        compiler_params=pltpu.CompilerParams(
            collective_id=0, has_side_effects=True, vmem_limit_bytes=60 * 1024 * 1024
        ),
        name="mixer_and_experts",
    )(*[operands[name] for name in OPERANDS])
    in_hbm = [pl.BlockSpec(memory_space=pltpu.HBM)] * 3
    stream, state, act = pl.pallas_call(
        finish,
        out_shape=results,
        in_specs=in_hbm,
        out_specs=in_hbm,
        scratch_shapes=[VMEM(r.shape, r.dtype) for r in results] + [dma((6,))],
        compiler_params=pltpu.CompilerParams(vmem_limit_bytes=60 * 1024 * 1024),
        name="results",
    )(*made)
    return (stream, state[None], act[None])


def solution(mesh):
    placed = (
        P("req", None, "mp"),
        P("req", None, "mp"),
        P(None, "mp"),
        P("mp"),
        P("mp", None),
        P(None, "mp"),
        P("mp"),
        P(None, "mp"),
        P("mp"),
        P("req", None, "mp"),
        P("req", None, "mp"),
        P(),
        P("mp", "req"),
        P(("req", "mp"), None),
        P(),
        P("req", None),
        P("req", None),
        P("req", None, "mp"),
        P("req", None, "mp"),
    )
    return jax.shard_map(
        local,
        mesh=mesh,
        in_specs=placed,
        out_specs=(P(("req", "mp"), None), P("req", None, "mp"), P("req", None, "mp")),
        check_vma=False,
    )
```
